128 devices in a mesh: seq: 16 (over y, x), mp: 8 (over z, core).
Axes of the slice: x: 4, y: 4, z: 4, core: 2. Of those that a mesh axis runs over, the one named last changes fastest.
Arguments:
- residual_activations: bfloat16 [16384, 4096], P('seq', 'mp'), may hold values from -6 to 6
- prelayer_gain_vector: bfloat16 [4096], replicated, may hold values from 0.099609375 to 1.8984375
- gating_projection: bfloat16 [4096], replicated, may hold values from -0.25 to 0.25
- asker_projection: bfloat16 [4096, 8192], P(None, 'mp'), may hold values from -0.09375 to 0.09375
- lookup_projection: bfloat16 [4096, 1024], P(None, 'mp'), may hold values from -0.09375 to 0.09375
- content_projection: bfloat16 [4096, 1024], P(None, 'mp'), may hold values from -0.09375 to 0.09375
- final_projection: bfloat16 [8192, 4096], P(None, 'mp'), may hold values from -0.0625 to 0.0625
- logit_sharpness: float32 [64], P('mp'), may hold values from 1 to 64
- selection_table: int32 [16, 256], P('seq'), may hold values from 0 to 1023, as said below
- dispatched_tally_table: int32 [16, 16], replicated, may hold values from 0 to 16, as said below
Outputs:
- blended: bfloat16 [16384, 4096], P('seq', 'mp')
The draws below stay inside these ranges and needn't reach their ends.
Inputs may be any that keep to these rules, and one draw needn't show every extreme that they name: `dispatched_tally_table`: entry [s, d] counts the routed tokens of source shard s whose compacted place falls to owner d: the compacted sequence lists all routed tokens in sequence order and is dealt in blocks of 8 places, block b to owner b mod 16. Every entry is a multiple of 8, and every column sums to 128. `selection_table`: row s lists in increasing order the distinct local indices of the routed tokens of source shard s, as many as row s of dispatched_tally_table sums to, and zeros after them.
All inputs are finite; a program needn't handle non-finite values.
Results may differ from the reference program's by a relative error of at most 0.0059.
Values may be sent and summed in bfloat16 or wider, within the bound.
No kernel may reach another device: no remote copies, remote signals or barrier semaphores. Data moves between devices by JAX's collectives and lax.ppermute only.
A program may use at most 64 MiB of HBM per device.

```python
import math
import jax
import jax.numpy as jnp
from jax import lax

D = 4096
HEADS = 64
SHARED_KV_COUNT = 8
PER_HEAD_DIM = 128
SRC_DEV = 1024
PICK = 256
BLOCK = 8
SEQ_LEN = 16384
ROUTED = 2048
N_SEQ = 16


def routing_tables(key):
    halves = N_SEQ // 2
    order = jax.random.permutation(jax.random.fold_in(key, 101), N_SEQ)
    amount = jax.random.randint(jax.random.fold_in(key, 102), (halves,), 0, N_SEQ + 1)
    amount = amount.at[0].set(N_SEQ)
    shares = jnp.concatenate([N_SEQ + amount, N_SEQ - amount]).astype(jnp.int32)
    spans = jnp.zeros((N_SEQ,), jnp.int32).at[order].set(shares)
    prefix = (jnp.cumsum(spans) - spans).astype(jnp.int32)
    owners = jnp.arange(N_SEQ, dtype=jnp.int32)
    first = (owners[None, :] - prefix[:, None]) % N_SEQ
    landed = jnp.maximum(spans[:, None] - first + N_SEQ - 1, 0) // N_SEQ
    return (spans, (landed * BLOCK).astype(jnp.int32))


def draw_dispatched_tally_table(key, part):
    spans, counts = routing_tables(key)
    return counts


def draw_selection_table(key, part):
    spans, counts = routing_tables(key)
    key = jax.random.fold_in(key, 7)
    shard_keys = jax.random.split(key, N_SEQ)

    def one_shard(shard_key, amount):
        ranks = jax.random.permutation(shard_key, SRC_DEV)
        marked = ranks < amount
        indices = jnp.arange(SRC_DEV, dtype=jnp.int32)
        ordering = jnp.argsort(jnp.where(marked, indices, indices + SRC_DEV))
        listed = ordering[:PICK].astype(jnp.int32)
        return jnp.where(jnp.arange(PICK) < amount, listed, 0).astype(jnp.int32)
    return jax.vmap(one_shard)(shard_keys, spans * BLOCK)


def draw_logit_sharpness(key, part):
    key = jax.random.fold_in(key, 3)
    values = jnp.exp(jax.random.uniform(key, (HEADS,), jnp.float32, 0.0, math.log(6.0)))
    return values


def block_levels(key, shape, pieces, smallest, top_value):
    loudness = 1.0
    for position, shards_of in pieces:
        steps = jax.random.uniform(jax.random.fold_in(jax.random.fold_in(key, 6), position), (shards_of,), jnp.float32, smallest / len(pieces), top_value / len(pieces))
        loudness = loudness * jnp.repeat(jnp.exp(steps), shape[position] // shards_of).reshape((-1,) + (1,) * (len(shape) - 1 - position))
    return loudness


def normal_values(rng, dims, width, limit, cuts=(), held_as=jnp.bfloat16):
    gain = block_levels(rng, dims, cuts, -0.22, 0.18) if cuts else 1.0
    values = jax.random.normal(rng, dims, jnp.float32) * width * gain
    return jnp.minimum(jnp.maximum(values, -limit), limit).astype(held_as)


def setup_inputs(seed: int = 0) -> dict:
    key_list = jax.random.split(jax.random.key(seed), 11)
    residual_activations = normal_values(key_list[0], (SEQ_LEN, D), 1.0, 6.0, ((0, 16), (1, 8)))
    prelayer_gain_vector = jnp.clip(1.0 + 0.18 * jax.random.normal(key_list[1], (D,), jnp.float32), 0.099609375, 1.8984375).astype(jnp.bfloat16)
    gating_projection = normal_values(key_list[2], (D,), (D // 9) ** -0.5, 0.25)
    asker_projection = normal_values(key_list[3], (D, HEADS * PER_HEAD_DIM), D ** -0.5, 0.09375, ((1, 8),))
    lookup_projection = normal_values(key_list[4], (D, SHARED_KV_COUNT * PER_HEAD_DIM), D ** -0.5, 0.09375, ((1, 8),))
    content_projection = normal_values(key_list[5], (D, SHARED_KV_COUNT * PER_HEAD_DIM), D ** -0.5, 0.09375, ((1, 8),))
    final_projection = normal_values(key_list[6], (HEADS * PER_HEAD_DIM, D), (HEADS * PER_HEAD_DIM) ** -0.5, 0.0625, ((1, 8),))
    logit_sharpness = draw_logit_sharpness(jax.random.fold_in(key_list[10], 71), 0)
    selection_table = draw_selection_table(jax.random.fold_in(key_list[10], 71), 0)
    dispatched_tally_table = draw_dispatched_tally_table(jax.random.fold_in(key_list[10], 71), 0)
    return dict(residual_activations=residual_activations, prelayer_gain_vector=prelayer_gain_vector, gating_projection=gating_projection, asker_projection=asker_projection, lookup_projection=lookup_projection, content_projection=content_projection, final_projection=final_projection, logit_sharpness=logit_sharpness, selection_table=selection_table, dispatched_tally_table=dispatched_tally_table)


def reference(residual_activations, prelayer_gain_vector, gating_projection, asker_projection, lookup_projection, content_projection, final_projection, logit_sharpness, selection_table, dispatched_tally_table):
    sent = lax.optimization_barrier(jnp.sum(dispatched_tally_table, axis=1)).astype(jnp.int32)
    start = (jnp.cumsum(sent) - sent).astype(jnp.int32)
    places = jnp.arange(ROUTED, dtype=jnp.int32)
    source = lax.optimization_barrier(jnp.sum((start[None, :] + sent[None, :] <= places[:, None]).astype(jnp.int32), axis=1))
    offset = (places - start[source]).astype(jnp.int32)
    token_rows = (source * SRC_DEV + selection_table[source, offset]).astype(jnp.int32)
    chosen = residual_activations[token_rows]
    gate = jax.nn.sigmoid(jnp.dot(chosen, gating_projection, preferred_element_type=jnp.float32))
    widened = chosen.astype(jnp.float32)
    inverse = lax.rsqrt(lax.optimization_barrier(jnp.mean(widened * widened, axis=1, keepdims=True)) + 1e-05)
    normed = (widened * inverse * prelayer_gain_vector.astype(jnp.float32)).astype(jnp.bfloat16)
    query = jnp.dot(normed, asker_projection, preferred_element_type=jnp.float32).astype(jnp.bfloat16)
    keys = jnp.dot(normed, lookup_projection, preferred_element_type=jnp.float32).astype(jnp.bfloat16)
    values = jnp.dot(normed, content_projection, preferred_element_type=jnp.float32).astype(jnp.bfloat16)
    asker_cluster = HEADS // SHARED_KV_COUNT
    query_heads = query.reshape(ROUTED, SHARED_KV_COUNT, asker_cluster, PER_HEAD_DIM).transpose(1, 0, 2, 3)
    key_heads = keys.reshape(ROUTED, SHARED_KV_COUNT, PER_HEAD_DIM).transpose(1, 0, 2)
    value_heads = values.reshape(ROUTED, SHARED_KV_COUNT, PER_HEAD_DIM).transpose(1, 0, 2)
    gating_multipliers = logit_sharpness.astype(jnp.float32).reshape(SHARED_KV_COUNT, asker_cluster) / math.sqrt(PER_HEAD_DIM)
    allowed = places[None, :] <= places[:, None]

    def one_head(item):
        query_part, key_part, value_part, scale_part = item
        score = jnp.einsum('qgd,kd->gqk', query_part.astype(jnp.float32), key_part.astype(jnp.float32))
        score = jnp.where(allowed[None], score * scale_part[:, None, None], -1e+30)
        highest = lax.optimization_barrier(jnp.max(score, axis=2, keepdims=True))
        weights = jnp.where(allowed[None], jnp.exp(score - highest), 0.0)
        totals = lax.optimization_barrier(jnp.sum(weights, axis=2))
        rounded = lax.optimization_barrier(weights.astype(jnp.bfloat16))
        mixed = jnp.einsum('gqk,kd->qgd', rounded.astype(jnp.float32), value_part.astype(jnp.float32))
        return (mixed / totals.T[:, :, None]).astype(jnp.bfloat16)
    head_results = lax.map(one_head, (query_heads, key_heads, value_heads, gating_multipliers))
    attended = head_results.transpose(1, 0, 2, 3).reshape(ROUTED, HEADS * PER_HEAD_DIM)
    projected = jnp.dot(attended, final_projection, preferred_element_type=jnp.float32)
    delta = (gate[:, None] * projected).astype(jnp.bfloat16)
    return residual_activations.astype(jnp.float32).at[token_rows].add(delta.astype(jnp.float32)).astype(jnp.bfloat16)
```

```python
import functools
import math

import jax
import jax.numpy as jnp
from jax import lax
from jax.experimental import pallas as pl
from jax.experimental.pallas import tpu as pltpu
from jax.sharding import PartitionSpec as P

NSEQ = 16
NMP = 8
BLOCK = 8
OWNED = 128
SLOTS = 256
SRC = 1024
FEAT = 512
WIDTH = 4096
HEAD = 128
GROUP = 8
MIB = 1 << 20

VMEM = pl.BlockSpec(memory_space=pltpu.VMEM)
SMEM = pl.BlockSpec(memory_space=pltpu.SMEM)
F32 = jnp.float32
BF16 = jnp.bfloat16


def params(mib):
    return pltpu.CompilerParams(vmem_limit_bytes=mib * MIB)


def cost(flops, bytes_accessed, transcendentals=0):
    return pl.CostEstimate(flops=flops, bytes_accessed=bytes_accessed, transcendentals=transcendentals)


def own_span(tally, shard):
    row = lax.broadcasted_iota(jnp.int32, (NSEQ, NSEQ), 0)
    before = jnp.sum(jnp.where(row < shard, tally, 0))
    mine = jnp.sum(jnp.where(row == shard, tally, 0))
    return before // BLOCK, mine


def pick_kernel(tally_ref, select_ref, rows_ref, out_ref):
    first, count = own_span(tally_ref[...], lax.axis_index("seq"))
    listed = select_ref[...]
    slot = lax.broadcasted_iota(jnp.int32, (1, SLOTS), 1)
    listed = jnp.where(slot < count, listed, -1).astype(F32)
    column = jnp.broadcast_to(listed, (128, SLOTS)).T
    lane = lax.broadcasted_iota(jnp.int32, (SLOTS, 128), 1).astype(F32)
    hot = jnp.concatenate(
        [(column == lane + float(128 * k)).astype(F32) for k in range(SRC // 128)], axis=1
    ).astype(BF16)
    picked = jnp.dot(hot, rows_ref[...], preferred_element_type=F32)
    for j in range(SLOTS // BLOCK):
        owner = lax.rem(first + j, NSEQ)
        out_ref[owner, j // NSEQ] = picked[BLOCK * j : BLOCK * (j + 1)].astype(BF16)


def table_kernel(tally_ref, table_ref):
    shard = lax.axis_index("seq")
    starts = []
    start = jnp.int32(0)
    for s in range(NSEQ):
        starts.append(start)
        table_ref[0, s] = start
        total = jnp.int32(0)
        for d in range(NSEQ):
            total = total + tally_ref[s, d]
        start = start + total // BLOCK
    starts.append(start)
    for i in range(NSEQ):
        block = i * NSEQ + shard
        source = jnp.int32(0)
        begin = jnp.int32(0)
        for s in range(1, NSEQ):
            past = starts[s] <= block
            source = jnp.where(past, s, source)
            begin = jnp.where(past, starts[s], begin)
        table_ref[1, i] = source
        table_ref[2, i] = (block - begin) // NSEQ


def compact_kernel(table_ref, in_ref, out_ref):
    for i in range(0, NSEQ, 2):
        pair = [
            in_ref[table_ref[1, k], table_ref[2, k]].astype(F32) for k in (i, i + 1)
        ]
        out_ref[BLOCK * i : BLOCK * (i + 2)] = jnp.concatenate(pair, axis=0).astype(BF16)


def block_of(k):
    me = lax.axis_index("mp")
    chip = lax.rem(me // 2 + (4 - k // 2), 4)
    core = lax.rem(lax.rem(me, 2) + k % 2, 2)
    return chip * 2 + core


def pair_kernel(gain_ref, keys_ref, values_ref, *refs):
    blocks, (normed_ref, pair_ref) = refs[:NMP], refs[NMP:]
    squares = jnp.zeros((OWNED, 128), F32)
    for k in range(NMP):
        wide = blocks[k][...].astype(F32)
        square = wide * wide
        for c in range(FEAT // 128):
            squares = squares + square[:, 128 * c : 128 * (c + 1)]
    inverse = lax.rsqrt(jnp.sum(squares, axis=1, keepdims=True) / WIDTH + 1e-05)
    keys = jnp.zeros((OWNED, HEAD), F32)
    values = jnp.zeros((OWNED, HEAD), F32)
    for k in range(NMP):
        m = block_of(k)
        rows = pl.ds(pl.multiple_of(m * FEAT, FEAT), FEAT)
        normed = (blocks[k][...].astype(F32) * inverse * gain_ref[m]).astype(BF16)
        normed_ref[k] = normed
        keys = keys + jnp.dot(normed, keys_ref[rows, :], preferred_element_type=F32)
        values = values + jnp.dot(normed, values_ref[rows, :], preferred_element_type=F32)
    keys = keys.astype(BF16)
    values = values.astype(BF16)
    for d in range(NSEQ):
        pair_ref[d, :, :HEAD] = keys
        pair_ref[d, :, HEAD:] = values


def query_kernel(normed_ref, weight_ref, gate_weight_ref, *refs):
    blocks, (query_ref, gate_ref) = refs[:NMP], refs[NMP:]
    total = jnp.zeros((OWNED, GROUP * HEAD), F32)
    routed = jnp.zeros((OWNED, FEAT), F32)
    for k in range(NMP):
        m = block_of(k)
        rows = pl.ds(pl.multiple_of(m * FEAT, FEAT), FEAT)
        total = total + jnp.dot(normed_ref[k], weight_ref[rows, :], preferred_element_type=F32)
        routed = routed + blocks[k][...].astype(F32) * gate_weight_ref[m]
    query_ref[...] = total.astype(BF16)
    gate_ref[...] = jnp.broadcast_to(
        jax.nn.sigmoid(jnp.sum(routed, axis=1, keepdims=True)), (OWNED, 128)
    )


def attention_kernel(sharp_ref, query_ref, pair_ref, out_ref):
    shard = lax.axis_index("seq")
    step = 4 * BLOCK
    rows = GROUP * step
    many = NSEQ * step
    scale = jnp.concatenate(
        [jnp.full((step, 1), sharp_ref[h] * (math.log2(math.e) / math.sqrt(HEAD)), F32) for h in range(GROUP)],
        axis=0,
    )
    q_row = lax.rem(lax.broadcasted_iota(jnp.int32, (rows, 1), 0), step)
    q_place = (q_row // BLOCK * NSEQ + shard) * BLOCK + q_row % BLOCK
    k_row = lax.broadcasted_iota(jnp.int32, (1, many), 1)
    k_place = ((k_row % step) // BLOCK * NSEQ + k_row // step) * BLOCK + k_row % BLOCK
    allowed = k_place <= q_place
    for j in range(4):
        here = slice(step * j, step * (j + 1))
        query = jnp.concatenate(
            [query_ref[here, HEAD * h : HEAD * (h + 1)] for h in range(GROUP)], axis=0
        )
        scores = []
        best = None
        for c in range(j + 1):
            keys = pair_ref[:, step * c : step * (c + 1), :HEAD].reshape(many, HEAD)
            score = lax.dot_general(
                query, keys, (((1,), (1,)), ((), ())), preferred_element_type=F32
            )
            if c == j:
                score = jnp.where(allowed, score, -1e30)
            scores.append(score)
            top = jnp.max(score, axis=1, keepdims=True)
            best = top if best is None else jnp.maximum(best, top)
        offset = best * scale
        total = jnp.zeros((rows, 1), F32)
        mixed = jnp.zeros((rows, HEAD), F32)
        for c in range(j + 1):
            weight = jnp.exp2(scores[c] * scale - offset)
            total = total + jnp.sum(weight, axis=1, keepdims=True)
            values = pair_ref[:, step * c : step * (c + 1), HEAD:].reshape(many, HEAD)
            mixed = mixed + jnp.dot(weight.astype(BF16), values, preferred_element_type=F32)
        mixed = (mixed / total).astype(BF16)
        for h in range(GROUP):
            out_ref[here, HEAD * h : HEAD * (h + 1)] = mixed[step * h : step * (h + 1)]


def project_kernel(table_ref, gate_ref, weight_ref, *refs):
    blocks, (out_ref, delta_ref) = refs[:NMP], refs[NMP:]
    shard = lax.axis_index("seq")
    wide = GROUP * HEAD
    total = jnp.zeros((OWNED, FEAT), F32)
    for k in range(NMP):
        m = block_of(k)
        rows = pl.ds(pl.multiple_of(m * wide, wide), wide)
        total = total + jnp.dot(blocks[k][...], weight_ref[rows, :], preferred_element_type=F32)
    delta = total * gate_ref[:, :1]
    for i in range(NSEQ):
        delta_ref[i] = delta[BLOCK * i : BLOCK * (i + 1)]
    for s in range(NSEQ):
        first = table_ref[0, s]
        counter = lax.rem(shard + NSEQ * NSEQ - first, NSEQ)
        for half in range(2):
            place = jnp.minimum((first + counter) // NSEQ + half, NSEQ - 1)
            out_ref[s, half] = delta_ref[place].astype(BF16)


def blend_kernel(tally_ref, select_ref, rows_ref, back_ref, out_ref, update_ref):
    first, count = own_span(tally_ref[...], lax.axis_index("seq"))
    for j in range(0, SLOTS // BLOCK, 2):
        pair = [
            back_ref[lax.rem(first + k, NSEQ), k // NSEQ].astype(F32) for k in (j, j + 1)
        ]
        update_ref[BLOCK * j : BLOCK * (j + 2)] = jnp.concatenate(pair, axis=0).astype(BF16)
    slot = lax.broadcasted_iota(jnp.int32, (1, SLOTS), 1)
    listed = jnp.where(slot < count, select_ref[...], -1)
    token = lax.broadcasted_iota(jnp.int32, (SRC, 1), 0)
    hot = (listed == token).astype(F32).astype(BF16)
    added = jnp.dot(hot, update_ref[...], preferred_element_type=F32)
    out_ref[...] = (rows_ref[...].astype(F32) + added).astype(BF16)


def z_step(array, steps):
    pairs = [(z * 2 + c, (z + steps) % 4 * 2 + c) for z in range(4) for c in range(2)]
    return lax.ppermute(array, "mp", pairs)


def other_core(array):
    return lax.ppermute(array, "mp", [(m, m ^ 1) for m in range(NMP)])


def gather_mp(array):
    chips = {0: array, 1: z_step(array, 1), 3: z_step(array, 3), 2: z_step(array, 2)}
    out = []
    for k in range(4):
        out += [chips[k], other_core(chips[k])]
    return out


def shape(dims, dtype=BF16):
    return jax.ShapeDtypeStruct(dims, dtype)


def on_device(
    residual_activations,
    prelayer_gain_vector,
    gating_projection,
    asker_projection,
    lookup_projection,
    content_projection,
    final_projection,
    logit_sharpness,
    selection_table,
    dispatched_tally_table,
):
    gain = prelayer_gain_vector.astype(F32).reshape(NMP, 1, FEAT)
    gate_weight = gating_projection.astype(F32).reshape(NMP, 1, FEAT)
    outgoing = pl.pallas_call(
        pick_kernel,
        out_shape=shape((NSEQ, 2, BLOCK, FEAT)),
        in_specs=[VMEM] * 3,
        out_specs=VMEM,
        compiler_params=params(16),
        name="pick",
    )(dispatched_tally_table, selection_table, residual_activations)
    table = pl.pallas_call(
        table_kernel,
        out_shape=shape((3, NSEQ), jnp.int32),
        in_specs=[SMEM],
        out_specs=SMEM,
        compiler_params=params(4),
        name="table",
    )(dispatched_tally_table)
    incoming = lax.all_to_all(outgoing, "seq", split_axis=0, concat_axis=0, tiled=True)
    tokens = pl.pallas_call(
        compact_kernel,
        out_shape=shape((OWNED, FEAT)),
        in_specs=[SMEM, VMEM],
        out_specs=VMEM,
        compiler_params=params(4),
        name="compact",
    )(table, incoming)
    blocks = gather_mp(tokens)
    normed, pair = pl.pallas_call(
        pair_kernel,
        out_shape=(shape((NMP, OWNED, FEAT)), shape((NSEQ, OWNED, 2 * HEAD))),
        in_specs=[VMEM] * (3 + NMP),
        out_specs=(VMEM, VMEM),
        compiler_params=params(16),
        cost_estimate=cost(2 * OWNED * WIDTH * 2 * HEAD, 4 * MIB),
        name="pair",
    )(gain, lookup_projection, content_projection, *blocks)
    pairs = lax.all_to_all(pair, "seq", split_axis=0, concat_axis=0, tiled=True)
    query, gate = pl.pallas_call(
        query_kernel,
        out_shape=(shape((OWNED, GROUP * HEAD)), shape((OWNED, 128), F32)),
        in_specs=[VMEM] * (3 + NMP),
        out_specs=(VMEM, VMEM),
        compiler_params=params(24),
        cost_estimate=cost(2 * OWNED * WIDTH * GROUP * HEAD, 10 * MIB),
        name="query",
    )(normed, asker_projection, gate_weight, *blocks)
    attended = pl.pallas_call(
        attention_kernel,
        out_shape=shape((OWNED, GROUP * HEAD)),
        in_specs=[SMEM, VMEM, VMEM],
        out_specs=VMEM,
        compiler_params=params(24),
        name="attend",
    )(logit_sharpness, query, pairs)
    heads = gather_mp(attended)
    outgoing_back = pl.pallas_call(
        project_kernel,
        out_shape=shape((NSEQ, 2, BLOCK, FEAT)),
        in_specs=[SMEM] + [VMEM] * (2 + NMP),
        out_specs=VMEM,
        scratch_shapes=[pltpu.VMEM((NSEQ, BLOCK, FEAT), F32)],
        compiler_params=params(24),
        name="project",
    )(table, gate, final_projection, *heads)
    back = lax.all_to_all(outgoing_back, "seq", split_axis=0, concat_axis=0, tiled=True)
    return pl.pallas_call(
        blend_kernel,
        out_shape=shape((SRC, FEAT)),
        in_specs=[VMEM] * 4,
        out_specs=VMEM,
        scratch_shapes=[pltpu.VMEM((SLOTS, FEAT), BF16)],
        compiler_params=params(24),
        name="blend",
    )(dispatched_tally_table, selection_table, residual_activations, back)


def solution(mesh):
    placed = (
        P("seq", "mp"),
        P(),
        P(),
        P(None, "mp"),
        P(None, "mp"),
        P(None, "mp"),
        P(None, "mp"),
        P("mp"),
        P("seq", None),
        P(),
    )
    return jax.shard_map(
        on_device, mesh=mesh, in_specs=placed, out_specs=P("seq", "mp"), check_vma=False
    )
```

```python
import functools
import math

import jax
import jax.numpy as jnp
from jax import lax
from jax.experimental import pallas as pl
from jax.experimental.pallas import tpu as pltpu
from jax.sharding import PartitionSpec as P

NSEQ = 16
NMP = 8
BLOCK = 8
OWNED = 128
SLOTS = 256
SRC = 1024
FEAT = 512
WIDTH = 4096
HEAD = 128
GROUP = 8
MIB = 1 << 20

VMEM = pl.BlockSpec(memory_space=pltpu.VMEM)
SMEM = pl.BlockSpec(memory_space=pltpu.SMEM)
HBM = pl.BlockSpec(memory_space=pltpu.HBM)
ANY = pl.BlockSpec(memory_space=pl.ANY)
F32 = jnp.float32
BF16 = jnp.bfloat16


def params(mib):
    return pltpu.CompilerParams(vmem_limit_bytes=mib * MIB)


def cost(flops, bytes_accessed, transcendentals=0):
    return pl.CostEstimate(flops=flops, bytes_accessed=bytes_accessed, transcendentals=transcendentals)


def own_span(tally, shard):
    row = lax.broadcasted_iota(jnp.int32, (NSEQ, NSEQ), 0)
    before = jnp.sum(jnp.where(row < shard, tally, 0))
    mine = jnp.sum(jnp.where(row == shard, tally, 0))
    return before // BLOCK, mine


def pick_kernel(tally_hbm, select_hbm, rows_hbm, out_ref, tally_ref, select_ref, rows_ref, sems):
    copies = [
        pltpu.make_async_copy(source, target, sems.at[k])
        for k, (source, target) in enumerate(
            ((tally_hbm, tally_ref), (select_hbm, select_ref), (rows_hbm, rows_ref))
        )
    ]
    for copy in copies:
        copy.start()
    copies[0].wait()
    copies[1].wait()
    first, count = own_span(tally_ref[...], lax.axis_index("seq"))
    listed = select_ref[...]
    slot = lax.broadcasted_iota(jnp.int32, (1, SLOTS), 1)
    listed = jnp.where(slot < count, listed, -1).astype(F32)
    column = jnp.broadcast_to(listed, (128, SLOTS)).T
    lane = lax.broadcasted_iota(jnp.int32, (SLOTS, 128), 1).astype(F32)
    hot = jnp.concatenate(
        [(column == lane + float(128 * k)).astype(F32) for k in range(SRC // 128)], axis=1
    ).astype(BF16)
    copies[2].wait()
    picked = jnp.dot(hot, rows_ref[...], preferred_element_type=F32)
    for j in range(SLOTS // BLOCK):
        owner = lax.rem(first + j, NSEQ)
        out_ref[owner, j // NSEQ] = picked[BLOCK * j : BLOCK * (j + 1)].astype(BF16)


def load_kernel(count, *refs):
    sources, targets, done_ref, sems = refs[:count], refs[-2 - count : -2], refs[-2], refs[-1]
    copies = [pltpu.make_async_copy(a, b, sems.at[k]) for k, (a, b) in enumerate(zip(sources, targets))]
    for copy in copies:
        copy.start()
    for copy in copies:
        copy.wait()
    done_ref[...] = jnp.zeros_like(done_ref)


def in_hbm(array):
    return pltpu.with_memory_space_constraint(array, pltpu.HBM)


def in_vmem(array):
    return pltpu.with_memory_space_constraint(array, pltpu.VMEM)


def load(arrays, after, name):
    count = len(arrays)
    return pl.pallas_call(
        functools.partial(load_kernel, count),
        out_shape=[pltpu.VMEM(a.shape, a.dtype) for a in arrays] + [pltpu.VMEM((8, 128), F32)],
        in_specs=[HBM] * count + [ANY],
        out_specs=[VMEM] * (count + 1),
        scratch_shapes=[pltpu.SemaphoreType.DMA((count,))],
        compiler_params=params(8),
        cost_estimate=cost(0, sum(a.size for a in arrays) * 2),
        name=name,
    )(*map(in_hbm, arrays), after)


def prep_kernel(tally_ref, gain_ref, gate_ref, table_ref, gain_out, gate_out):
    gain_out[...] = gain_ref[...]
    gate_out[...] = gate_ref[...]
    shard = lax.axis_index("seq")
    starts = []
    start = jnp.int32(0)
    for s in range(NSEQ):
        starts.append(start)
        table_ref[0, s] = start
        total = jnp.int32(0)
        for d in range(NSEQ):
            total = total + tally_ref[s, d]
        start = start + total // BLOCK
    starts.append(start)
    for i in range(NSEQ):
        block = i * NSEQ + shard
        source = jnp.int32(0)
        begin = jnp.int32(0)
        for s in range(1, NSEQ):
            past = starts[s] <= block
            source = jnp.where(past, s, source)
            begin = jnp.where(past, starts[s], begin)
        table_ref[1, i] = source
        table_ref[2, i] = (block - begin) // NSEQ


def compact_kernel(table_ref, in_ref, out_ref):
    for i in range(0, NSEQ, 2):
        pair = [
            in_ref[table_ref[1, k], table_ref[2, k]].astype(F32) for k in (i, i + 1)
        ]
        out_ref[BLOCK * i : BLOCK * (i + 2)] = jnp.concatenate(pair, axis=0).astype(BF16)


def block_of(k):
    me = lax.axis_index("mp")
    chip = lax.rem(me // 2 + (4 - k // 2), 4)
    core = lax.rem(lax.rem(me, 2) + k % 2, 2)
    return chip * 2 + core


def pair_kernel(gain_ref, keys_hbm, values_hbm, *refs):
    blocks, (normed_ref, pair_ref, keys_ref, values_ref, sems) = refs[:NMP], refs[NMP:]
    copies = [
        pltpu.make_async_copy(keys_hbm, keys_ref, sems.at[0]),
        pltpu.make_async_copy(values_hbm, values_ref, sems.at[1]),
    ]
    for copy in copies:
        copy.start()
    squares = jnp.zeros((OWNED, 128), F32)
    for k in range(NMP):
        wide = blocks[k][...].astype(F32)
        square = wide * wide
        for c in range(FEAT // 128):
            squares = squares + square[:, 128 * c : 128 * (c + 1)]
    inverse = lax.rsqrt(jnp.sum(squares, axis=1, keepdims=True) / WIDTH + 1e-05)
    for copy in copies:
        copy.wait()
    keys = jnp.zeros((OWNED, HEAD), F32)
    values = jnp.zeros((OWNED, HEAD), F32)
    for k in range(NMP):
        m = block_of(k)
        rows = pl.ds(pl.multiple_of(m * FEAT, FEAT), FEAT)
        normed = (blocks[k][...].astype(F32) * inverse * gain_ref[m]).astype(BF16)
        normed_ref[k] = normed
        keys = keys + jnp.dot(normed, keys_ref[rows, :], preferred_element_type=F32)
        values = values + jnp.dot(normed, values_ref[rows, :], preferred_element_type=F32)
    keys = keys.astype(BF16)
    values = values.astype(BF16)
    for d in range(NSEQ):
        pair_ref[d, :, :HEAD] = keys
        pair_ref[d, :, HEAD:] = values


def query_kernel(normed_ref, weight_ref, gate_weight_ref, *refs):
    blocks, (query_ref, gate_ref, held_ref, sems) = refs[:NMP], refs[NMP:]
    copies = []
    for k in range(NMP):
        rows = pl.ds(pl.multiple_of(block_of(k) * FEAT, FEAT), FEAT)
        copies.append(pltpu.make_async_copy(weight_ref.at[rows, :], held_ref.at[k], sems.at[k]))
        copies[k].start()
    total = jnp.zeros((OWNED, GROUP * HEAD), F32)
    routed = jnp.zeros((OWNED, FEAT), F32)
    for k in range(NMP):
        routed = routed + blocks[k][...].astype(F32) * gate_weight_ref[block_of(k)]
        copies[k].wait()
        total = total + jnp.dot(normed_ref[k], held_ref[k], preferred_element_type=F32)
    query_ref[...] = total.astype(BF16)
    gate_ref[...] = jnp.broadcast_to(
        jax.nn.sigmoid(jnp.sum(routed, axis=1, keepdims=True)), (OWNED, 128)
    )


def attention_kernel(sharp_ref, query_ref, pair_ref, out_ref):
    shard = lax.axis_index("seq")
    step = 4 * BLOCK
    rows = GROUP * step
    many = NSEQ * step
    scale = jnp.concatenate(
        [jnp.full((step, 1), sharp_ref[h] * (math.log2(math.e) / math.sqrt(HEAD)), F32) for h in range(GROUP)],
        axis=0,
    )
    q_row = lax.rem(lax.broadcasted_iota(jnp.int32, (rows, 1), 0), step)
    q_place = (q_row // BLOCK * NSEQ + shard) * BLOCK + q_row % BLOCK
    k_row = lax.broadcasted_iota(jnp.int32, (1, many), 1)
    k_place = ((k_row % step) // BLOCK * NSEQ + k_row // step) * BLOCK + k_row % BLOCK
    allowed = k_place <= q_place
    for j in range(4):
        here = slice(step * j, step * (j + 1))
        query = jnp.concatenate(
            [query_ref[here, HEAD * h : HEAD * (h + 1)] for h in range(GROUP)], axis=0
        )
        scores = []
        best = None
        for c in range(j + 1):
            keys = pair_ref[:, step * c : step * (c + 1), :HEAD].reshape(many, HEAD)
            score = lax.dot_general(
                query, keys, (((1,), (1,)), ((), ())), preferred_element_type=F32
            )
            if c == j:
                score = jnp.where(allowed, score, -1e30)
            scores.append(score)
            top = jnp.max(score, axis=1, keepdims=True)
            best = top if best is None else jnp.maximum(best, top)
        offset = best * scale
        total = jnp.zeros((rows, 1), F32)
        mixed = jnp.zeros((rows, HEAD), F32)
        for c in range(j + 1):
            weight = jnp.exp2(scores[c] * scale - offset)
            total = total + jnp.sum(weight, axis=1, keepdims=True)
            values = pair_ref[:, step * c : step * (c + 1), HEAD:].reshape(many, HEAD)
            mixed = mixed + jnp.dot(weight.astype(BF16), values, preferred_element_type=F32)
        mixed = (mixed / total).astype(BF16)
        for h in range(GROUP):
            out_ref[here, HEAD * h : HEAD * (h + 1)] = mixed[step * h : step * (h + 1)]


def project_kernel(table_ref, gate_ref, weight_ref, *refs):
    blocks, (out_ref, delta_ref) = refs[:NMP], refs[NMP:]
    shard = lax.axis_index("seq")
    wide = GROUP * HEAD
    total = jnp.zeros((OWNED, FEAT), F32)
    for k in range(NMP):
        m = block_of(k)
        rows = pl.ds(pl.multiple_of(m * wide, wide), wide)
        total = total + jnp.dot(blocks[k][...], weight_ref[rows, :], preferred_element_type=F32)
    delta = total * gate_ref[:, :1]
    for i in range(NSEQ):
        delta_ref[i] = delta[BLOCK * i : BLOCK * (i + 1)]
    for s in range(NSEQ):
        first = table_ref[0, s]
        counter = lax.rem(shard + NSEQ * NSEQ - first, NSEQ)
        for half in range(2):
            place = jnp.minimum((first + counter) // NSEQ + half, NSEQ - 1)
            out_ref[s, half] = delta_ref[place].astype(BF16)


def blend_kernel(tally_ref, select_ref, rows_ref, back_ref, out_ref, update_ref):
    first, count = own_span(tally_ref[...], lax.axis_index("seq"))
    for j in range(0, SLOTS // BLOCK, 2):
        pair = [
            back_ref[lax.rem(first + k, NSEQ), k // NSEQ].astype(F32) for k in (j, j + 1)
        ]
        update_ref[BLOCK * j : BLOCK * (j + 2)] = jnp.concatenate(pair, axis=0).astype(BF16)
    slot = lax.broadcasted_iota(jnp.int32, (1, SLOTS), 1)
    listed = jnp.where(slot < count, select_ref[...], -1)
    token = lax.broadcasted_iota(jnp.int32, (SRC, 1), 0)
    hot = (listed == token).astype(F32).astype(BF16)
    added = jnp.dot(hot, update_ref[...], preferred_element_type=F32)
    out_ref[...] = (rows_ref[...].astype(F32) + added).astype(BF16)


def z_step(array, steps):
    pairs = [(z * 2 + c, (z + steps) % 4 * 2 + c) for z in range(4) for c in range(2)]
    return lax.ppermute(array, "mp", pairs)


def other_core(array):
    return lax.ppermute(array, "mp", [(m, m ^ 1) for m in range(NMP)])


def gather_mp(array, before=None):
    chips = {0: array, 1: z_step(array, 1), 3: z_step(array, 3), 2: z_step(array, 2)}
    if before is not None:
        chips[3], _ = lax.optimization_barrier((chips[3], before))
    out = []
    for k in range(4):
        out += [chips[k], other_core(chips[k])]
    return out


def shape(dims, dtype=BF16):
    return jax.ShapeDtypeStruct(dims, dtype)


def on_device(
    residual_activations,
    prelayer_gain_vector,
    gating_projection,
    asker_projection,
    lookup_projection,
    content_projection,
    final_projection,
    logit_sharpness,
    selection_table,
    dispatched_tally_table,
):
    outgoing = pl.pallas_call(
        pick_kernel,
        out_shape=pltpu.VMEM((NSEQ, 2, BLOCK, FEAT), BF16),
        in_specs=[HBM] * 3,
        out_specs=VMEM,
        scratch_shapes=[
            pltpu.VMEM((NSEQ, NSEQ), jnp.int32),
            pltpu.VMEM((1, SLOTS), jnp.int32),
            pltpu.VMEM((SRC, FEAT), BF16),
            pltpu.SemaphoreType.DMA((3,)),
        ],
        compiler_params=params(16),
        name="pick",
    )(in_hbm(dispatched_tally_table), in_hbm(selection_table), in_hbm(residual_activations))
    table, gain, gate_weight = pl.pallas_call(
        prep_kernel,
        out_shape=(
            shape((3, NSEQ), jnp.int32),
            pltpu.VMEM((NMP, 1, FEAT), F32),
            pltpu.VMEM((NMP, 1, FEAT), F32),
        ),
        in_specs=[SMEM, VMEM, VMEM],
        out_specs=(SMEM, VMEM, VMEM),
        compiler_params=params(4),
        name="prep",
    )(
        dispatched_tally_table,
        prelayer_gain_vector.astype(F32).reshape(NMP, 1, FEAT),
        gating_projection.astype(F32).reshape(NMP, 1, FEAT),
    )
    incoming = lax.all_to_all(outgoing, "seq", split_axis=0, concat_axis=0, tiled=True)
    tokens = pl.pallas_call(
        compact_kernel,
        out_shape=shape((OWNED, FEAT)),
        in_specs=[SMEM, VMEM],
        out_specs=VMEM,
        compiler_params=params(4),
        name="compact",
    )(table, incoming)
    blocks = gather_mp(tokens)
    normed, pair = pl.pallas_call(
        pair_kernel,
        out_shape=(pltpu.VMEM((NMP, OWNED, FEAT), BF16), pltpu.VMEM((NSEQ, OWNED, 2 * HEAD), BF16)),
        in_specs=[VMEM, HBM, HBM] + [VMEM] * NMP,
        out_specs=(VMEM, VMEM),
        scratch_shapes=[
            pltpu.VMEM((WIDTH, HEAD), BF16),
            pltpu.VMEM((WIDTH, HEAD), BF16),
            pltpu.SemaphoreType.DMA((2,)),
        ],
        compiler_params=params(16),
        cost_estimate=cost(2 * OWNED * WIDTH * 2 * HEAD, 4 * MIB),
        name="pair",
    )(gain, in_hbm(lookup_projection), in_hbm(content_projection), *blocks)
    pairs = lax.all_to_all(pair, "seq", split_axis=0, concat_axis=0, tiled=True)
    query, gate = pl.pallas_call(
        query_kernel,
        out_shape=(shape((OWNED, GROUP * HEAD)), shape((OWNED, 128), F32)),
        in_specs=[VMEM, HBM, VMEM] + [VMEM] * NMP,
        out_specs=(VMEM, VMEM),
        scratch_shapes=[
            pltpu.VMEM((NMP, FEAT, GROUP * HEAD), BF16),
            pltpu.SemaphoreType.DMA((NMP,)),
        ],
        compiler_params=params(24),
        cost_estimate=cost(2 * OWNED * WIDTH * GROUP * HEAD, 10 * MIB),
        name="query",
    )(normed, in_hbm(asker_projection), gate_weight, *blocks)
    attended = pl.pallas_call(
        attention_kernel,
        out_shape=shape((OWNED, GROUP * HEAD)),
        in_specs=[SMEM, VMEM, VMEM],
        out_specs=VMEM,
        compiler_params=params(24),
        name="attend",
    )(logit_sharpness, query, pairs)
    final, loaded = load((final_projection,), attended, "load")
    heads = gather_mp(attended, loaded)
    outgoing_back = pl.pallas_call(
        project_kernel,
        out_shape=pltpu.VMEM((NSEQ, 2, BLOCK, FEAT), BF16),
        in_specs=[SMEM] + [VMEM] * (2 + NMP),
        out_specs=VMEM,
        scratch_shapes=[pltpu.VMEM((NSEQ, BLOCK, FEAT), F32)],
        compiler_params=params(24),
        name="project",
    )(table, gate, final, *heads)
    back = lax.all_to_all(outgoing_back, "seq", split_axis=0, concat_axis=0, tiled=True)
    return pl.pallas_call(
        blend_kernel,
        out_shape=shape((SRC, FEAT)),
        in_specs=[VMEM] * 4,
        out_specs=VMEM,
        scratch_shapes=[pltpu.VMEM((SLOTS, FEAT), BF16)],
        compiler_params=params(24),
        name="blend",
    )(dispatched_tally_table, selection_table, residual_activations, back)


def solution(mesh):
    placed = (
        P("seq", "mp"),
        P(),
        P(),
        P(None, "mp"),
        P(None, "mp"),
        P(None, "mp"),
        P(None, "mp"),
        P("mp"),
        P("seq", None),
        P(),
    )
    return jax.shard_map(
        on_device, mesh=mesh, in_specs=placed, out_specs=P("seq", "mp"), check_vma=False
    )
```

```python
import functools
import math

import jax
import jax.numpy as jnp
from jax import lax
from jax.experimental import pallas as pl
from jax.experimental.pallas import tpu as pltpu
from jax.sharding import PartitionSpec as P

NSEQ = 16
NMP = 8
BLOCK = 8
OWNED = 128
SLOTS = 256
SRC = 1024
FEAT = 512
WIDTH = 4096
HEAD = 128
GROUP = 8
MIB = 1 << 20

VMEM = pl.BlockSpec(memory_space=pltpu.VMEM)
SMEM = pl.BlockSpec(memory_space=pltpu.SMEM)
HBM = pl.BlockSpec(memory_space=pltpu.HBM)
ANY = pl.BlockSpec(memory_space=pl.ANY)
F32 = jnp.float32
BF16 = jnp.bfloat16


def params(mib):
    return pltpu.CompilerParams(vmem_limit_bytes=mib * MIB)


def cost(flops, bytes_accessed, transcendentals=0):
    return pl.CostEstimate(flops=flops, bytes_accessed=bytes_accessed, transcendentals=transcendentals)


def own_span(tally, shard):
    row = lax.broadcasted_iota(jnp.int32, (NSEQ, NSEQ), 0)
    before = jnp.sum(jnp.where(row < shard, tally, 0))
    mine = jnp.sum(jnp.where(row == shard, tally, 0))
    return before // BLOCK, mine


def pick_kernel(tally_hbm, select_hbm, rows_hbm, out_ref, tally_ref, select_ref, rows_ref, sems):
    copies = [
        pltpu.make_async_copy(source, target, sems.at[k])
        for k, (source, target) in enumerate(
            ((tally_hbm, tally_ref), (select_hbm, select_ref), (rows_hbm, rows_ref))
        )
    ]
    for copy in copies:
        copy.start()
    copies[0].wait()
    copies[1].wait()
    first, count = own_span(tally_ref[...], lax.axis_index("seq"))
    listed = select_ref[...]
    slot = lax.broadcasted_iota(jnp.int32, (1, SLOTS), 1)
    listed = jnp.where(slot < count, listed, -1).astype(F32)
    column = jnp.broadcast_to(listed, (128, SLOTS)).T
    lane = lax.broadcasted_iota(jnp.int32, (SLOTS, 128), 1).astype(F32)
    hot = jnp.concatenate(
        [(column == lane + float(128 * k)).astype(F32) for k in range(SRC // 128)], axis=1
    ).astype(BF16)
    copies[2].wait()
    picked = jnp.dot(hot, rows_ref[...], preferred_element_type=F32)
    for j in range(SLOTS // BLOCK):
        owner = lax.rem(first + j, NSEQ)
        out_ref[owner, j // NSEQ] = picked[BLOCK * j : BLOCK * (j + 1)].astype(BF16)


def load_kernel(count, *refs):
    sources, targets, done_ref, sems = refs[:count], refs[-2 - count : -2], refs[-2], refs[-1]
    copies = [pltpu.make_async_copy(a, b, sems.at[k]) for k, (a, b) in enumerate(zip(sources, targets))]
    for copy in copies:
        copy.start()
    for copy in copies:
        copy.wait()
    done_ref[...] = jnp.zeros_like(done_ref)


def in_hbm(array):
    return pltpu.with_memory_space_constraint(array, pltpu.HBM)


def in_vmem(array):
    return pltpu.with_memory_space_constraint(array, pltpu.VMEM)


def load(arrays, after, name):
    count = len(arrays)
    return pl.pallas_call(
        functools.partial(load_kernel, count),
        out_shape=[pltpu.VMEM(a.shape, a.dtype) for a in arrays] + [pltpu.VMEM((8, 128), F32)],
        in_specs=[HBM] * count + [ANY],
        out_specs=[VMEM] * (count + 1),
        scratch_shapes=[pltpu.SemaphoreType.DMA((count,))],
        compiler_params=params(8),
        cost_estimate=cost(0, sum(a.size for a in arrays) * 2),
        name=name,
    )(*map(in_hbm, arrays), after)


def prep_kernel(tally_ref, gain_ref, gate_ref, table_ref, gain_out, gate_out):
    gain_out[...] = gain_ref[...]
    gate_out[...] = gate_ref[...]
    shard = lax.axis_index("seq")
    starts = []
    start = jnp.int32(0)
    for s in range(NSEQ):
        starts.append(start)
        table_ref[0, s] = start
        total = jnp.int32(0)
        for d in range(NSEQ):
            total = total + tally_ref[s, d]
        start = start + total // BLOCK
    starts.append(start)
    for i in range(NSEQ):
        block = i * NSEQ + shard
        source = jnp.int32(0)
        begin = jnp.int32(0)
        for s in range(1, NSEQ):
            past = starts[s] <= block
            source = jnp.where(past, s, source)
            begin = jnp.where(past, starts[s], begin)
        table_ref[1, i] = source
        table_ref[2, i] = (block - begin) // NSEQ


def compact_kernel(table_ref, in_ref, out_ref):
    for i in range(0, NSEQ, 2):
        pair = [
            in_ref[table_ref[1, k], table_ref[2, k]].astype(F32) for k in (i, i + 1)
        ]
        out_ref[BLOCK * i : BLOCK * (i + 2)] = jnp.concatenate(pair, axis=0).astype(BF16)


def block_of(k):
    me = lax.axis_index("mp")
    chip = lax.rem(me // 2 + (4 - k // 2), 4)
    core = lax.rem(lax.rem(me, 2) + k % 2, 2)
    return chip * 2 + core


def project_in_kernel(gain_ref, gate_weight_ref, query_weight_ref, keys_ref, values_ref, *refs):
    blocks, (query_ref, gate_ref, pair_ref) = refs[:NMP], refs[NMP:]
    squares = jnp.zeros((OWNED, 128), F32)
    routed = jnp.zeros((OWNED, 128), F32)
    for k in range(NMP):
        wide = blocks[k][...].astype(F32)
        square = wide * wide
        weighted = wide * gate_weight_ref[block_of(k)]
        for c in range(FEAT // 128):
            squares = squares + square[:, 128 * c : 128 * (c + 1)]
            routed = routed + weighted[:, 128 * c : 128 * (c + 1)]
    inverse = lax.rsqrt(jnp.sum(squares, axis=1, keepdims=True) / WIDTH + 1e-05)
    gate_ref[...] = jnp.broadcast_to(
        jax.nn.sigmoid(jnp.sum(routed, axis=1, keepdims=True)), (OWNED, 128)
    )
    query = jnp.zeros((OWNED, GROUP * HEAD), F32)
    keys = jnp.zeros((OWNED, HEAD), F32)
    values = jnp.zeros((OWNED, HEAD), F32)
    for k in range(NMP):
        m = block_of(k)
        rows = pl.ds(pl.multiple_of(m * FEAT, FEAT), FEAT)
        normed = (blocks[k][...].astype(F32) * inverse * gain_ref[m]).astype(BF16)
        keys = keys + jnp.dot(normed, keys_ref[rows, :], preferred_element_type=F32)
        values = values + jnp.dot(normed, values_ref[rows, :], preferred_element_type=F32)
        query = query + jnp.dot(normed, query_weight_ref[rows, :], preferred_element_type=F32)
    query_ref[...] = query.astype(BF16)
    keys = keys.astype(BF16)
    values = values.astype(BF16)
    for d in range(NSEQ):
        pair_ref[d, :, :HEAD] = keys
        pair_ref[d, :, HEAD:] = values


def attention_kernel(sharp_ref, query_ref, pair_ref, out_ref):
    shard = lax.axis_index("seq")
    step = 4 * BLOCK
    rows = GROUP * step
    many = NSEQ * step
    scale = jnp.concatenate(
        [jnp.full((step, 1), sharp_ref[h] * (math.log2(math.e) / math.sqrt(HEAD)), F32) for h in range(GROUP)],
        axis=0,
    )
    q_row = lax.rem(lax.broadcasted_iota(jnp.int32, (rows, 1), 0), step)
    q_place = (q_row // BLOCK * NSEQ + shard) * BLOCK + q_row % BLOCK
    k_row = lax.broadcasted_iota(jnp.int32, (1, many), 1)
    k_place = ((k_row % step) // BLOCK * NSEQ + k_row // step) * BLOCK + k_row % BLOCK
    allowed = k_place <= q_place
    for j in range(4):
        here = slice(step * j, step * (j + 1))
        query = jnp.concatenate(
            [query_ref[here, HEAD * h : HEAD * (h + 1)] for h in range(GROUP)], axis=0
        )
        scores = []
        best = None
        for c in range(j + 1):
            keys = pair_ref[:, step * c : step * (c + 1), :HEAD].reshape(many, HEAD)
            score = lax.dot_general(
                query, keys, (((1,), (1,)), ((), ())), preferred_element_type=F32
            )
            if c == j:
                score = jnp.where(allowed, score, -1e30)
            scores.append(score)
            top = jnp.max(score, axis=1, keepdims=True)
            best = top if best is None else jnp.maximum(best, top)
        offset = best * scale
        total = jnp.zeros((rows, 1), F32)
        mixed = jnp.zeros((rows, HEAD), F32)
        for c in range(j + 1):
            weight = jnp.exp2(scores[c] * scale - offset)
            total = total + jnp.sum(weight, axis=1, keepdims=True)
            values = pair_ref[:, step * c : step * (c + 1), HEAD:].reshape(many, HEAD)
            mixed = mixed + jnp.dot(weight.astype(BF16), values, preferred_element_type=F32)
        mixed = (mixed / total).astype(BF16)
        for h in range(GROUP):
            out_ref[here, HEAD * h : HEAD * (h + 1)] = mixed[step * h : step * (h + 1)]


def project_kernel(table_ref, gate_ref, weight_ref, *refs):
    blocks, (out_ref, delta_ref) = refs[:NMP], refs[NMP:]
    shard = lax.axis_index("seq")
    wide = GROUP * HEAD
    total = jnp.zeros((OWNED, FEAT), F32)
    for k in range(NMP):
        m = block_of(k)
        rows = pl.ds(pl.multiple_of(m * wide, wide), wide)
        total = total + jnp.dot(blocks[k][...], weight_ref[rows, :], preferred_element_type=F32)
    delta = total * gate_ref[:, :1]
    for i in range(NSEQ):
        delta_ref[i] = delta[BLOCK * i : BLOCK * (i + 1)]
    for s in range(NSEQ):
        first = table_ref[0, s]
        counter = lax.rem(shard + NSEQ * NSEQ - first, NSEQ)
        for half in range(2):
            place = jnp.minimum((first + counter) // NSEQ + half, NSEQ - 1)
            out_ref[s, half] = delta_ref[place].astype(BF16)


def blend_kernel(tally_ref, select_ref, rows_ref, back_ref, out_ref, update_ref):
    first, count = own_span(tally_ref[...], lax.axis_index("seq"))
    for j in range(0, SLOTS // BLOCK, 2):
        pair = [
            back_ref[lax.rem(first + k, NSEQ), k // NSEQ].astype(F32) for k in (j, j + 1)
        ]
        update_ref[BLOCK * j : BLOCK * (j + 2)] = jnp.concatenate(pair, axis=0).astype(BF16)
    slot = lax.broadcasted_iota(jnp.int32, (1, SLOTS), 1)
    listed = jnp.where(slot < count, select_ref[...], -1)
    token = lax.broadcasted_iota(jnp.int32, (SRC, 1), 0)
    hot = (listed == token).astype(F32).astype(BF16)
    added = jnp.dot(hot, update_ref[...], preferred_element_type=F32)
    out_ref[...] = (rows_ref[...].astype(F32) + added).astype(BF16)


def z_step(array, steps):
    pairs = [(z * 2 + c, (z + steps) % 4 * 2 + c) for z in range(4) for c in range(2)]
    return lax.ppermute(array, "mp", pairs)


def other_core(array):
    return lax.ppermute(array, "mp", [(m, m ^ 1) for m in range(NMP)])


def hand_on_kernel(in_ref, token_ref, out_ref):
    out_ref[...] = in_ref[...]


def hand_on(array, token):
    return pl.pallas_call(
        hand_on_kernel,
        out_shape=pltpu.VMEM(array.shape, array.dtype),
        in_specs=[VMEM, ANY],
        out_specs=VMEM,
        compiler_params=params(4),
        name="hand_on",
    )(array, token)


def gather_mp(array, token):
    chips = {0: array, 1: z_step(array, 1), 3: z_step(array, 3), 2: z_step(array, 2)}
    other = {0: other_core(array)}
    for k in (3, 1, 2):
        other[k] = other_core(hand_on(chips[k], token) if k == 3 else chips[k])
    return [part[k] for k in range(4) for part in (chips, other)]


def shape(dims, dtype=BF16):
    return jax.ShapeDtypeStruct(dims, dtype)


def on_device(
    residual_activations,
    prelayer_gain_vector,
    gating_projection,
    asker_projection,
    lookup_projection,
    content_projection,
    final_projection,
    logit_sharpness,
    selection_table,
    dispatched_tally_table,
):
    outgoing = pl.pallas_call(
        pick_kernel,
        out_shape=pltpu.VMEM((NSEQ, 2, BLOCK, FEAT), BF16),
        in_specs=[HBM] * 3,
        out_specs=VMEM,
        scratch_shapes=[
            pltpu.VMEM((NSEQ, NSEQ), jnp.int32),
            pltpu.VMEM((1, SLOTS), jnp.int32),
            pltpu.VMEM((SRC, FEAT), BF16),
            pltpu.SemaphoreType.DMA((3,)),
        ],
        compiler_params=params(16),
        name="pick",
    )(in_hbm(dispatched_tally_table), in_hbm(selection_table), in_hbm(residual_activations))
    table, gain, gate_weight = pl.pallas_call(
        prep_kernel,
        out_shape=(
            shape((3, NSEQ), jnp.int32),
            pltpu.VMEM((NMP, 1, FEAT), F32),
            pltpu.VMEM((NMP, 1, FEAT), F32),
        ),
        in_specs=[SMEM, VMEM, VMEM],
        out_specs=(SMEM, VMEM, VMEM),
        compiler_params=params(4),
        name="prep",
    )(
        dispatched_tally_table,
        prelayer_gain_vector.astype(F32).reshape(NMP, 1, FEAT),
        gating_projection.astype(F32).reshape(NMP, 1, FEAT),
    )
    incoming = lax.all_to_all(outgoing, "seq", split_axis=0, concat_axis=0, tiled=True)
    tokens = pl.pallas_call(
        compact_kernel,
        out_shape=shape((OWNED, FEAT)),
        in_specs=[SMEM, VMEM],
        out_specs=VMEM,
        compiler_params=params(4),
        name="compact",
    )(table, incoming)
    asker, lookup, content, loaded = load(
        (asker_projection, lookup_projection, content_projection), tokens, "load_in"
    )
    blocks = gather_mp(tokens, loaded)
    query, gate, pair = pl.pallas_call(
        project_in_kernel,
        out_shape=(
            pltpu.VMEM((OWNED, GROUP * HEAD), BF16),
            pltpu.VMEM((OWNED, 128), F32),
            pltpu.VMEM((NSEQ, OWNED, 2 * HEAD), BF16),
        ),
        in_specs=[VMEM] * (5 + NMP),
        out_specs=(VMEM, VMEM, VMEM),
        compiler_params=params(16),
        cost_estimate=cost(2 * OWNED * WIDTH * 10 * HEAD, 4 * MIB),
        name="project_in",
    )(gain, gate_weight, asker, lookup, content, *blocks)
    pairs = lax.all_to_all(pair, "seq", split_axis=0, concat_axis=0, tiled=True)
    attended = pl.pallas_call(
        attention_kernel,
        out_shape=shape((OWNED, GROUP * HEAD)),
        in_specs=[SMEM, VMEM, VMEM],
        out_specs=VMEM,
        compiler_params=params(24),
        name="attend",
    )(logit_sharpness, query, pairs)
    final, loaded = load((final_projection,), attended, "load_out")
    heads = gather_mp(attended, loaded)
    outgoing_back = pl.pallas_call(
        project_kernel,
        out_shape=pltpu.VMEM((NSEQ, 2, BLOCK, FEAT), BF16),
        in_specs=[SMEM] + [VMEM] * (2 + NMP),
        out_specs=VMEM,
        scratch_shapes=[pltpu.VMEM((NSEQ, BLOCK, FEAT), F32)],
        compiler_params=params(24),
        name="project",
    )(table, gate, final, *heads)
    back = lax.all_to_all(outgoing_back, "seq", split_axis=0, concat_axis=0, tiled=True)
    return pl.pallas_call(
        blend_kernel,
        out_shape=shape((SRC, FEAT)),
        in_specs=[VMEM] * 4,
        out_specs=VMEM,
        scratch_shapes=[pltpu.VMEM((SLOTS, FEAT), BF16)],
        compiler_params=params(24),
        name="blend",
    )(dispatched_tally_table, selection_table, residual_activations, back)


def solution(mesh):
    placed = (
        P("seq", "mp"),
        P(),
        P(),
        P(None, "mp"),
        P(None, "mp"),
        P(None, "mp"),
        P(None, "mp"),
        P("mp"),
        P("seq", None),
        P(),
    )
    return jax.shard_map(
        on_device, mesh=mesh, in_specs=placed, out_specs=P("seq", "mp"), check_vma=False
    )
```

```python
import functools
import math

import jax
import jax.numpy as jnp
from jax import lax
from jax.experimental import pallas as pl
from jax.experimental.pallas import tpu as pltpu
from jax.sharding import PartitionSpec as P

NSEQ = 16
NMP = 8
BLOCK = 8
OWNED = 128
SLOTS = 256
SRC = 1024
FEAT = 512
WIDTH = 4096
HEAD = 128
GROUP = 8
MIB = 1 << 20

VMEM = pl.BlockSpec(memory_space=pltpu.VMEM)
SMEM = pl.BlockSpec(memory_space=pltpu.SMEM)
HBM = pl.BlockSpec(memory_space=pltpu.HBM)
ANY = pl.BlockSpec(memory_space=pl.ANY)
F32 = jnp.float32
BF16 = jnp.bfloat16


def params(mib):
    return pltpu.CompilerParams(vmem_limit_bytes=mib * MIB)


def cost(flops, bytes_accessed, transcendentals=0):
    return pl.CostEstimate(flops=flops, bytes_accessed=bytes_accessed, transcendentals=transcendentals)


def own_span(tally, shard):
    row = lax.broadcasted_iota(jnp.int32, (NSEQ, NSEQ), 0)
    before = jnp.sum(jnp.where(row < shard, tally, 0))
    mine = jnp.sum(jnp.where(row == shard, tally, 0))
    return before // BLOCK, mine


def deal(tally, shard):
    row = lax.broadcasted_iota(jnp.int32, (NSEQ, NSEQ), 0)
    lane = lax.broadcasted_iota(jnp.int32, (NSEQ, NSEQ), 1)
    total = jnp.right_shift(jnp.sum(tally, axis=1, keepdims=True), 3)
    across = jnp.sum(jnp.where(row == lane, total, 0), axis=0, keepdims=True)
    start = jnp.sum(jnp.where(lane < row, across, 0), axis=1, keepdims=True)
    start_across = jnp.sum(jnp.where(row < lane, total, 0), axis=0, keepdims=True)
    block = lane[:1] * NSEQ + shard
    past = start <= block
    source = jnp.sum(past.astype(jnp.int32), axis=0, keepdims=True) - 1
    begin = jnp.max(jnp.where(past, start, 0), axis=0, keepdims=True)
    return jnp.concatenate([start_across, source, jnp.right_shift(block - begin, 4)], axis=0)


def pick_kernel(tally_hbm, select_hbm, rows_hbm, out_ref, table_ref, tally_ref, select_ref, rows_ref, sems):
    parts = rows_ref.shape[0]
    wide = SRC // parts
    copies = [
        pltpu.make_async_copy(tally_hbm, tally_ref, sems.at[parts]),
        pltpu.make_async_copy(select_hbm, select_ref, sems.at[parts + 1]),
    ] + [
        pltpu.make_async_copy(rows_hbm.at[pl.ds(wide * p, wide), :], rows_ref.at[p], sems.at[p])
        for p in range(parts)
    ]
    for copy in copies:
        copy.start()
    copies[0].wait()
    copies[1].wait()
    tally = tally_ref[...]
    shard = lax.axis_index("seq")
    first, count = own_span(tally, shard)
    table_ref[...] = deal(tally, shard)
    listed = select_ref[...]
    slot = lax.broadcasted_iota(jnp.int32, (1, SLOTS), 1)
    listed = jnp.where(slot < count, listed, -1).astype(F32)
    column = jnp.broadcast_to(listed, (128, SLOTS)).T
    lane = lax.broadcasted_iota(jnp.int32, (SLOTS, 128), 1).astype(F32)
    picked = jnp.zeros((SLOTS, FEAT), F32)
    for p in range(parts):
        hot = jnp.concatenate(
            [(column == lane + float(wide * p + 128 * k)).astype(F32) for k in range(wide // 128)],
            axis=1,
        ).astype(BF16)
        copies[2 + p].wait()
        picked = picked + jnp.dot(hot, rows_ref[p], preferred_element_type=F32)
    for j in range(SLOTS // BLOCK):
        owner = lax.rem(first + j, NSEQ)
        out_ref[owner, j // NSEQ] = picked[BLOCK * j : BLOCK * (j + 1)].astype(BF16)


def load_kernel(count, *refs):
    sources, targets, done_ref, sems = refs[:count], refs[-2 - count : -2], refs[-2], refs[-1]
    copies = [pltpu.make_async_copy(a, b, sems.at[k]) for k, (a, b) in enumerate(zip(sources, targets))]
    for copy in copies:
        copy.start()
    for copy in copies:
        copy.wait()
    done_ref[...] = jnp.zeros_like(done_ref)


def in_hbm(array):
    return pltpu.with_memory_space_constraint(array, pltpu.HBM)


def in_vmem(array):
    return pltpu.with_memory_space_constraint(array, pltpu.VMEM)


def load(arrays, after, name):
    count = len(arrays)
    return pl.pallas_call(
        functools.partial(load_kernel, count),
        out_shape=[pltpu.VMEM(a.shape, a.dtype) for a in arrays] + [pltpu.VMEM((8, 128), F32)],
        in_specs=[HBM] * count + [ANY],
        out_specs=[VMEM] * (count + 1),
        scratch_shapes=[pltpu.SemaphoreType.DMA((count,))],
        compiler_params=params(8),
        cost_estimate=cost(0, sum(a.size for a in arrays) * 2),
        name=name,
    )(*map(in_hbm, arrays), after)


def compact_kernel(table_ref, in_ref, out_ref):
    for i in range(0, NSEQ, 2):
        pair = [
            in_ref[table_ref[1, k], table_ref[2, k]].astype(F32) for k in (i, i + 1)
        ]
        out_ref[BLOCK * i : BLOCK * (i + 2)] = jnp.concatenate(pair, axis=0).astype(BF16)


def block_of(k):
    me = lax.axis_index("mp")
    chip = lax.rem(me // 2 + (4 - k // 2), 4)
    core = lax.rem(lax.rem(me, 2) + k % 2, 2)
    return chip * 2 + core


def spread(packed_ref, spread_ref):
    wide = packed_ref[...].astype(F32)
    parts = FEAT // 128
    for r in range(WIDTH // 128):
        spread_ref[r // parts, r % parts : r % parts + 1] = wide[r : r + 1]


def project_in_kernel(gain_in, query_weight_ref, keys_ref, values_ref, *refs):
    blocks, (query_ref, pair_ref, gain_ref) = refs[:NMP], refs[NMP:]
    parts = FEAT // 128
    spread(gain_in, gain_ref)
    squares = jnp.zeros((OWNED, 128), F32)
    for k in range(NMP):
        for c in range(parts):
            wide = blocks[k][:, 128 * c : 128 * (c + 1)].astype(F32)
            squares = squares + wide * wide
    inverse = lax.rsqrt(jnp.sum(squares, axis=1, keepdims=True) / WIDTH + 1e-05)
    query = jnp.zeros((OWNED, GROUP * HEAD), F32)
    keys = jnp.zeros((OWNED, HEAD), F32)
    values = jnp.zeros((OWNED, HEAD), F32)
    for k in range(NMP):
        m = block_of(k)
        rows = pl.ds(pl.multiple_of(m * FEAT, FEAT), FEAT)
        gain = gain_ref[m]
        normed = jnp.concatenate(
            [
                (
                    blocks[k][:, 128 * c : 128 * (c + 1)].astype(F32) * inverse * gain[c : c + 1]
                ).astype(BF16)
                for c in range(parts)
            ],
            axis=1,
        )
        keys = keys + jnp.dot(normed, keys_ref[rows, :], preferred_element_type=F32)
        values = values + jnp.dot(normed, values_ref[rows, :], preferred_element_type=F32)
        query = query + jnp.dot(normed, query_weight_ref[rows, :], preferred_element_type=F32)
    query_ref[...] = query.astype(BF16)
    keys = keys.astype(BF16)
    values = values.astype(BF16)
    for d in range(NSEQ):
        pair_ref[d, :, :HEAD] = keys
        pair_ref[d, :, HEAD:] = values


def attention_kernel(sharp_ref, query_ref, pair_ref, out_ref):
    shard = lax.axis_index("seq")
    step = 4 * BLOCK
    rows = GROUP * step
    many = NSEQ * step
    scale = jnp.concatenate(
        [
            jnp.full((step, 1), sharp_ref[h] * (math.log2(math.e) / math.sqrt(HEAD)), F32)
            for h in range(GROUP)
        ],
        axis=0,
    )
    q_row = lax.rem(lax.broadcasted_iota(jnp.int32, (rows, 1), 0), step)
    q_place = (q_row // BLOCK * NSEQ + shard) * BLOCK + q_row % BLOCK
    k_row = lax.broadcasted_iota(jnp.int32, (1, many), 1)
    k_place = ((k_row % step) // BLOCK * NSEQ + k_row // step) * BLOCK + k_row % BLOCK
    allowed = k_place <= q_place

    def scores_of(j):
        query = jnp.concatenate(
            [query_ref[step * j : step * (j + 1), HEAD * h : HEAD * (h + 1)] for h in range(GROUP)],
            axis=0,
        )
        scores = []
        for c in range(j + 1):
            keys = pair_ref[:, step * c : step * (c + 1), :HEAD].reshape(many, HEAD)
            score = lax.dot_general(
                query, keys, (((1,), (1,)), ((), ())), preferred_element_type=F32
            )
            scores.append(jnp.where(allowed, score, -1e30) if c == j else score)
        return scores

    later = scores_of(3)
    for j in (3, 2, 1, 0):
        scores = later
        if j:
            later = scores_of(j - 1)
        best = functools.reduce(
            jnp.maximum, [jnp.max(score, axis=1, keepdims=True) for score in scores]
        )
        offset = best * scale
        total = jnp.zeros((rows, 1), F32)
        mixed = jnp.zeros((rows, HEAD), F32)
        for c, score in enumerate(scores):
            weight = jnp.exp2(score * scale - offset)
            total = total + jnp.sum(weight, axis=1, keepdims=True)
            values = pair_ref[:, step * c : step * (c + 1), HEAD:].reshape(many, HEAD)
            mixed = mixed + jnp.dot(weight.astype(BF16), values, preferred_element_type=F32)
        mixed = (mixed / total).astype(BF16)
        for h in range(GROUP):
            out_ref[step * j : step * (j + 1), HEAD * h : HEAD * (h + 1)] = mixed[
                step * h : step * (h + 1)
            ]


EARLY, MIDDLE, LAST = (0, 1), (2, 3, 4, 5, 6), (7,)


def head_sum(which, weight_ref, blocks):
    wide = GROUP * HEAD
    total = jnp.zeros((OWNED, FEAT), F32)
    for k, block in zip(which, blocks):
        rows = pl.ds(pl.multiple_of(block_of(k) * wide, wide), wide)
        total = total + jnp.dot(block[...], weight_ref[rows, :], preferred_element_type=F32)
    return total


def project_early_kernel(weight_ref, gate_in, *refs):
    tokens, heads, (total_ref, gate_ref, gate_weight_ref) = refs[:NMP], refs[NMP:-3], refs[-3:]
    spread(gate_in, gate_weight_ref)
    routed = jnp.zeros((OWNED, 128), F32)
    for k in range(NMP):
        weights = gate_weight_ref[block_of(k)]
        for c in range(FEAT // 128):
            routed = routed + tokens[k][:, 128 * c : 128 * (c + 1)].astype(F32) * weights[c : c + 1]
    gate_ref[...] = jnp.broadcast_to(
        jax.nn.sigmoid(jnp.sum(routed, axis=1, keepdims=True)), (OWNED, 128)
    )
    total_ref[...] = head_sum(EARLY, weight_ref, heads)


def project_middle_kernel(total_in, weight_ref, *refs):
    refs[-1][...] = total_in[...] + head_sum(MIDDLE, weight_ref, refs[:-1])


def project_last_kernel(table_ref, gate_ref, total_ref, weight_ref, *refs):
    blocks, (out_ref, delta_ref) = refs[:-2], refs[-2:]
    shard = lax.axis_index("seq")
    delta = (total_ref[...] + head_sum(LAST, weight_ref, blocks)) * gate_ref[:, :1]
    for i in range(NSEQ):
        delta_ref[i] = delta[BLOCK * i : BLOCK * (i + 1)]
    for s in range(NSEQ):
        first = table_ref[0, s]
        counter = lax.rem(shard + NSEQ * NSEQ - first, NSEQ)
        for half in range(2):
            place = jnp.minimum((first + counter) // NSEQ + half, NSEQ - 1)
            out_ref[s, half] = delta_ref[place].astype(BF16)


def blend_kernel(tally_ref, select_ref, rows_ref, back_ref, out_hbm, update_ref, out_ref, sems):
    first, count = own_span(tally_ref[...], lax.axis_index("seq"))
    for j in range(0, SLOTS // BLOCK, 2):
        pair = [
            back_ref[lax.rem(first + k, NSEQ), k // NSEQ].astype(F32) for k in (j, j + 1)
        ]
        update_ref[BLOCK * j : BLOCK * (j + 2)] = jnp.concatenate(pair, axis=0).astype(BF16)
    slot = lax.broadcasted_iota(jnp.int32, (1, SLOTS), 1)
    listed = jnp.where(slot < count, select_ref[...], -1)
    parts = out_ref.shape[0]
    wide = SRC // parts
    token = lax.broadcasted_iota(jnp.int32, (wide, 1), 0)
    copies = []
    for p in range(parts):
        here = slice(wide * p, wide * (p + 1))
        hot = (listed == token + wide * p).astype(F32).astype(BF16)
        added = jnp.dot(hot, update_ref[...], preferred_element_type=F32)
        out_ref[p] = (rows_ref[here].astype(F32) + added).astype(BF16)
        copies.append(pltpu.make_async_copy(out_ref.at[p], out_hbm.at[pl.ds(wide * p, wide), :], sems.at[p]))
        copies[p].start()
    for copy in copies:
        copy.wait()


def z_step(array, steps):
    pairs = [(z * 2 + c, (z + steps) % 4 * 2 + c) for z in range(4) for c in range(2)]
    return lax.ppermute(array, "mp", pairs)


def other_core(array):
    return lax.ppermute(array, "mp", [(m, m ^ 1) for m in range(NMP)])


def hand_on_kernel(in_ref, token_ref, out_ref):
    out_ref[...] = in_ref[...]


def hand_on(array, token):
    return pl.pallas_call(
        hand_on_kernel,
        out_shape=pltpu.VMEM(array.shape, array.dtype),
        in_specs=[VMEM, ANY],
        out_specs=VMEM,
        compiler_params=params(4),
        name="hand_on",
    )(array, token)


def z_blocks(array):
    return {0: array, 2: z_step(array, 1), 6: z_step(array, 3), 4: z_step(array, 2)}


def add_cores(blocks, token):
    for k in (6, 2, 4):
        blocks[k + 1] = other_core(hand_on(blocks[k], token) if k == 6 else blocks[k])


def shape(dims, dtype=BF16):
    return jax.ShapeDtypeStruct(dims, dtype)


def on_device(
    residual_activations,
    prelayer_gain_vector,
    gating_projection,
    asker_projection,
    lookup_projection,
    content_projection,
    final_projection,
    logit_sharpness,
    selection_table,
    dispatched_tally_table,
):
    outgoing, table = pl.pallas_call(
        pick_kernel,
        out_shape=(pltpu.VMEM((NSEQ, 2, BLOCK, FEAT), BF16), shape((3, NSEQ), jnp.int32)),
        in_specs=[HBM] * 3,
        out_specs=(VMEM, VMEM),
        scratch_shapes=[
            pltpu.VMEM((NSEQ, NSEQ), jnp.int32),
            pltpu.VMEM((1, SLOTS), jnp.int32),
            pltpu.VMEM((4, SRC // 4, FEAT), BF16),
            pltpu.SemaphoreType.DMA((6,)),
        ],
        compiler_params=params(16),
        name="pick",
    )(in_hbm(dispatched_tally_table), in_hbm(selection_table), in_hbm(residual_activations))
    incoming = lax.all_to_all(outgoing, "seq", split_axis=0, concat_axis=0, tiled=True)
    tokens = pl.pallas_call(
        compact_kernel,
        out_shape=shape((OWNED, FEAT)),
        in_specs=[SMEM, VMEM],
        out_specs=VMEM,
        compiler_params=params(4),
        name="compact",
    )(table, incoming)
    asker, lookup, content, loaded = load(
        (asker_projection, lookup_projection, content_projection), tokens, "load_in"
    )
    blocks = z_blocks(tokens)
    blocks[1] = other_core(tokens)
    add_cores(blocks, loaded)
    blocks = [blocks[k] for k in range(NMP)]
    query, pair = pl.pallas_call(
        project_in_kernel,
        out_shape=(
            pltpu.VMEM((OWNED, GROUP * HEAD), BF16),
            pltpu.VMEM((NSEQ, OWNED, 2 * HEAD), BF16),
        ),
        in_specs=[VMEM] * (4 + NMP),
        out_specs=[VMEM] * 2,
        scratch_shapes=[pltpu.VMEM((NMP, FEAT // 128, 128), F32)],
        compiler_params=params(16),
        cost_estimate=cost(2 * OWNED * WIDTH * 10 * HEAD, 4 * MIB),
        name="project_in",
    )(
        prelayer_gain_vector.reshape(WIDTH // 128, 128),
        asker,
        lookup,
        content,
        *blocks,
    )
    pairs = lax.all_to_all(pair, "seq", split_axis=0, concat_axis=0, tiled=True)

    attended = pl.pallas_call(
        attention_kernel,
        out_shape=shape((OWNED, GROUP * HEAD)),
        in_specs=[SMEM, VMEM, VMEM],
        out_specs=VMEM,
        compiler_params=params(24),
        name="attend",
    )(logit_sharpness, query, pairs)
    final, _ = load((final_projection,), attended, "load_out")
    heads = z_blocks(attended)
    heads[1] = other_core(attended)
    total, gate = pl.pallas_call(
        project_early_kernel,
        out_shape=(pltpu.VMEM((OWNED, FEAT), F32), pltpu.VMEM((OWNED, 128), F32)),
        in_specs=[VMEM] * (2 + NMP + len(EARLY)),
        out_specs=(VMEM, VMEM),
        scratch_shapes=[pltpu.VMEM((NMP, FEAT // 128, 128), F32)],
        compiler_params=params(16),
        name="project_early",
    )(final, gating_projection.reshape(WIDTH // 128, 128), *blocks, *(heads[k] for k in EARLY))
    add_cores(heads, total)
    total = pl.pallas_call(
        project_middle_kernel,
        out_shape=pltpu.VMEM((OWNED, FEAT), F32),
        in_specs=[VMEM] * (2 + len(MIDDLE)),
        out_specs=VMEM,
        compiler_params=params(16),
        name="project_middle",
    )(total, final, *(heads[k] for k in MIDDLE))
    outgoing_back = pl.pallas_call(
        project_last_kernel,
        out_shape=pltpu.VMEM((NSEQ, 2, BLOCK, FEAT), BF16),
        in_specs=[SMEM] + [VMEM] * (3 + len(LAST)),
        out_specs=VMEM,
        scratch_shapes=[pltpu.VMEM((NSEQ, BLOCK, FEAT), F32)],
        compiler_params=params(16),
        name="project_last",
    )(table, gate, total, final, *(heads[k] for k in LAST))
    back = lax.all_to_all(outgoing_back, "seq", split_axis=0, concat_axis=0, tiled=True)
    return pl.pallas_call(
        blend_kernel,
        out_shape=shape((SRC, FEAT)),
        in_specs=[VMEM] * 4,
        out_specs=HBM,
        scratch_shapes=[
            pltpu.VMEM((SLOTS, FEAT), BF16),
            pltpu.VMEM((4, SRC // 4, FEAT), BF16),
            pltpu.SemaphoreType.DMA((4,)),
        ],
        compiler_params=params(16),
        name="blend",
    )(dispatched_tally_table, selection_table, residual_activations, back)


def solution(mesh):
    placed = (
        P("seq", "mp"),
        P(),
        P(),
        P(None, "mp"),
        P(None, "mp"),
        P(None, "mp"),
        P(None, "mp"),
        P("mp"),
        P("seq", None),
        P(),
    )
    return jax.shard_map(
        on_device, mesh=mesh, in_specs=placed, out_specs=P("seq", "mp"), check_vma=False
    )
```

```python
import functools
import math

import jax
import jax.numpy as jnp
from jax import lax
from jax.experimental import pallas as pl
from jax.experimental.pallas import tpu as pltpu
from jax.sharding import PartitionSpec as P

NSEQ = 16
NMP = 8
BLOCK = 8
OWNED = 128
SLOTS = 256
SRC = 1024
FEAT = 512
WIDTH = 4096
HEAD = 128
GROUP = 8
MIB = 1 << 20

VMEM = pl.BlockSpec(memory_space=pltpu.VMEM)
SMEM = pl.BlockSpec(memory_space=pltpu.SMEM)
HBM = pl.BlockSpec(memory_space=pltpu.HBM)
ANY = pl.BlockSpec(memory_space=pl.ANY)
F32 = jnp.float32
BF16 = jnp.bfloat16


def params(mib):
    return pltpu.CompilerParams(vmem_limit_bytes=mib * MIB)


def cost(flops, bytes_accessed, transcendentals=0):
    return pl.CostEstimate(flops=flops, bytes_accessed=bytes_accessed, transcendentals=transcendentals)


def own_span(tally, shard):
    row = lax.broadcasted_iota(jnp.int32, (NSEQ, NSEQ), 0)
    before = jnp.sum(jnp.where(row < shard, tally, 0))
    mine = jnp.sum(jnp.where(row == shard, tally, 0))
    return before // BLOCK, mine


def deal(tally, shard):
    row = lax.broadcasted_iota(jnp.int32, (NSEQ, NSEQ), 0)
    lane = lax.broadcasted_iota(jnp.int32, (NSEQ, NSEQ), 1)
    total = jnp.right_shift(jnp.sum(tally, axis=1, keepdims=True), 3)
    across = jnp.sum(jnp.where(row == lane, total, 0), axis=0, keepdims=True)
    start = jnp.sum(jnp.where(lane < row, across, 0), axis=1, keepdims=True)
    start_across = jnp.sum(jnp.where(row < lane, total, 0), axis=0, keepdims=True)
    block = lane[:1] * NSEQ + shard
    past = start <= block
    source = jnp.sum(past.astype(jnp.int32), axis=0, keepdims=True) - 1
    begin = jnp.max(jnp.where(past, start, 0), axis=0, keepdims=True)
    return jnp.concatenate([start_across, source, jnp.right_shift(block - begin, 4)], axis=0)


def pick_kernel(
    tally_hbm, select_hbm, rows_hbm, sharp_hbm, out_ref, table_out, sharp_out, table_ref, tally_ref, select_ref, rows_ref, sems
):
    parts = rows_ref.shape[0]
    wide = SRC // parts
    copies = [
        pltpu.make_async_copy(tally_hbm, tally_ref, sems.at[parts]),
        pltpu.make_async_copy(select_hbm, select_ref, sems.at[parts + 1]),
    ] + [
        pltpu.make_async_copy(rows_hbm.at[pl.ds(wide * p, wide), :], rows_ref.at[p], sems.at[p])
        for p in range(parts)
    ]
    copies.append(pltpu.make_async_copy(sharp_hbm, sharp_out, sems.at[parts + 3]))
    for copy in copies:
        copy.start()
    copies[0].wait()
    copies[1].wait()
    tally = tally_ref[...]
    shard = lax.axis_index("seq")
    first, count = own_span(tally, shard)
    table_ref[...] = deal(tally, shard)
    dealt = pltpu.make_async_copy(table_ref, table_out, sems.at[parts + 2])
    dealt.start()
    listed = select_ref[...]
    slot = lax.broadcasted_iota(jnp.int32, (1, SLOTS), 1)
    listed = jnp.where(slot < count, listed, -1).astype(F32)
    column = jnp.broadcast_to(listed, (128, SLOTS)).T
    lane = lax.broadcasted_iota(jnp.int32, (SLOTS, 128), 1).astype(F32)
    picked = jnp.zeros((SLOTS, FEAT), F32)
    for p in range(parts):
        hot = jnp.concatenate(
            [(column == lane + float(wide * p + 128 * k)).astype(F32) for k in range(wide // 128)],
            axis=1,
        ).astype(BF16)
        copies[2 + p].wait()
        picked = picked + jnp.dot(hot, rows_ref[p], preferred_element_type=F32)
    for j in range(SLOTS // BLOCK):
        owner = lax.rem(first + j, NSEQ)
        out_ref[owner, j // NSEQ] = picked[BLOCK * j : BLOCK * (j + 1)].astype(BF16)
    dealt.wait()
    copies[-1].wait()


def in_hbm(array):
    return pltpu.with_memory_space_constraint(array, pltpu.HBM)


def block_rows(k, wide):
    return pl.ds(pl.multiple_of(block_of(k) * wide, wide), wide)


def fetch(source, target, sems, first, parts):
    wide = source.shape[0] // parts
    copies = [
        pltpu.make_async_copy(
            source.at[pl.ds(wide * p, wide), :], target.at[pl.ds(wide * p, wide), :], sems.at[first + p]
        )
        for p in range(parts)
    ]
    for copy in copies:
        copy.start()
    return copies


def load_in_kernel(keys_hbm, values_hbm, query_hbm, after_ref, keys_ref, values_ref, query_ref, done_ref, sems):
    copies = fetch(keys_hbm, keys_ref, sems, 0, 2)
    copies += fetch(values_hbm, values_ref, sems, 2, 2)
    copies += fetch(query_hbm, query_ref, sems, 4, 8)
    done_ref[...] = jnp.zeros_like(done_ref)
    for copy in copies:
        copy.wait()


def compact_kernel(table_ref, in_ref, out_ref):
    for i in range(0, NSEQ, 2):
        pair = [
            in_ref[table_ref[1, k], table_ref[2, k]].astype(F32) for k in (i, i + 1)
        ]
        out_ref[BLOCK * i : BLOCK * (i + 2)] = jnp.concatenate(pair, axis=0).astype(BF16)


def block_of(k):
    me = lax.axis_index("mp")
    chip = lax.rem(me // 2 + (4 - k // 2), 4)
    core = lax.rem(lax.rem(me, 2) + k % 2, 2)
    return chip * 2 + core


def spread(packed_ref, spread_ref):
    wide = packed_ref[...].astype(F32)
    parts = FEAT // 128
    for r in range(WIDTH // 128):
        spread_ref[r // parts, r % parts : r % parts + 1] = wide[r : r + 1]


def project_in_kernel(gain_in, query_weight_ref, keys_ref, values_ref, *refs):
    blocks, (query_ref, pair_ref, gain_ref) = refs[:NMP], refs[NMP:]
    parts = FEAT // 128
    spread(gain_in, gain_ref)
    squares = jnp.zeros((OWNED, 128), F32)
    for k in range(NMP):
        for c in range(parts):
            wide = blocks[k][:, 128 * c : 128 * (c + 1)].astype(F32)
            squares = squares + wide * wide
    inverse = lax.rsqrt(jnp.sum(squares, axis=1, keepdims=True) / WIDTH + 1e-05)
    query = jnp.zeros((OWNED, GROUP * HEAD), F32)
    keys = jnp.zeros((OWNED, HEAD), F32)
    values = jnp.zeros((OWNED, HEAD), F32)
    for k in range(NMP):
        m = block_of(k)
        rows = block_rows(k, FEAT)
        gain = gain_ref[m]
        normed = jnp.concatenate(
            [
                (
                    blocks[k][:, 128 * c : 128 * (c + 1)].astype(F32) * inverse * gain[c : c + 1]
                ).astype(BF16)
                for c in range(parts)
            ],
            axis=1,
        )
        keys = keys + jnp.dot(normed, keys_ref[rows, :], preferred_element_type=F32)
        values = values + jnp.dot(normed, values_ref[rows, :], preferred_element_type=F32)
        query = query + jnp.dot(normed, query_weight_ref[rows, :], preferred_element_type=F32)
    query_ref[...] = query.astype(BF16)
    keys = keys.astype(BF16)
    values = values.astype(BF16)
    for d in range(NSEQ):
        pair_ref[d, :, :HEAD] = keys
        pair_ref[d, :, HEAD:] = values


def attention_kernel(sharp_ref, query_ref, pair_ref, out_ref):
    shard = lax.axis_index("seq")
    step = 4 * BLOCK
    rows = GROUP * step
    many = NSEQ * step
    scale = jnp.concatenate(
        [
            jnp.full((step, 1), sharp_ref[h] * (math.log2(math.e) / math.sqrt(HEAD)), F32)
            for h in range(GROUP)
        ],
        axis=0,
    )
    q_row = lax.rem(lax.broadcasted_iota(jnp.int32, (rows, 1), 0), step)
    q_place = (q_row // BLOCK * NSEQ + shard) * BLOCK + q_row % BLOCK
    k_row = lax.broadcasted_iota(jnp.int32, (1, many), 1)
    k_place = ((k_row % step) // BLOCK * NSEQ + k_row // step) * BLOCK + k_row % BLOCK
    allowed = k_place <= q_place

    def scores_of(j):
        query = jnp.concatenate(
            [query_ref[step * j : step * (j + 1), HEAD * h : HEAD * (h + 1)] for h in range(GROUP)],
            axis=0,
        )
        scores = []
        for c in range(j + 1):
            keys = pair_ref[:, step * c : step * (c + 1), :HEAD].reshape(many, HEAD)
            score = lax.dot_general(
                query, keys, (((1,), (1,)), ((), ())), preferred_element_type=F32
            )
            scores.append(jnp.where(allowed, score, -1e30) if c == j else score)
        return scores

    later = scores_of(3)
    for j in (3, 2, 1, 0):
        scores = later
        if j:
            later = scores_of(j - 1)
        best = functools.reduce(
            jnp.maximum, [jnp.max(score, axis=1, keepdims=True) for score in scores]
        )
        offset = best * scale
        total = jnp.zeros((rows, 1), F32)
        mixed = jnp.zeros((rows, HEAD), F32)
        for c, score in enumerate(scores):
            weight = jnp.exp2(score * scale - offset)
            total = total + jnp.sum(weight, axis=1, keepdims=True)
            values = pair_ref[:, step * c : step * (c + 1), HEAD:].reshape(many, HEAD)
            mixed = mixed + jnp.dot(weight.astype(BF16), values, preferred_element_type=F32)
        mixed = (mixed / total).astype(BF16)
        for h in range(GROUP):
            out_ref[step * j : step * (j + 1), HEAD * h : HEAD * (h + 1)] = mixed[
                step * h : step * (h + 1)
            ]


MIDDLE, LAST = (1, 2, 3, 4, 5, 6), (7,)


def head_sum(which, weight_ref, blocks):
    wide = GROUP * HEAD
    total = jnp.zeros((OWNED, FEAT), F32)
    for k, block in zip(which, blocks):
        total = total + jnp.dot(
            block[...], weight_ref[block_rows(k, wide), :], preferred_element_type=F32
        )
    return total


def load_out_kernel(weight_hbm, tally_ref, select_ref, gate_in, own_ref, *refs):
    tokens, (weight_ref, total_ref, gate_ref, hot_ref, gate_weight_ref, sems) = refs[:NMP], refs[NMP:]
    copies = fetch(weight_hbm, weight_ref, sems, 0, 8)
    spread(gate_in, gate_weight_ref)
    routed = jnp.zeros((OWNED, 128), F32)
    for k in range(NMP):
        weights = gate_weight_ref[block_of(k)]
        for c in range(FEAT // 128):
            routed = routed + tokens[k][:, 128 * c : 128 * (c + 1)].astype(F32) * weights[c : c + 1]
    gate_ref[...] = jnp.broadcast_to(
        jax.nn.sigmoid(jnp.sum(routed, axis=1, keepdims=True)), (OWNED, 128)
    )
    first, count = own_span(tally_ref[...], lax.axis_index("seq"))
    slot = lax.broadcasted_iota(jnp.int32, (1, SLOTS), 1)
    listed = jnp.where(slot < count, select_ref[...], -1)
    token = lax.broadcasted_iota(jnp.int32, (SRC, 1), 0)
    hot_ref[...] = (listed == token).astype(F32).astype(BF16)
    for copy in copies:
        copy.wait()
    total_ref[...] = head_sum((0,), weight_ref, (own_ref,))


def project_middle_kernel(total_in, weight_ref, *refs):
    refs[-1][...] = total_in[...] + head_sum(MIDDLE, weight_ref, refs[:-1])


def project_last_kernel(table_ref, gate_ref, total_ref, weight_ref, *refs):
    blocks, (out_ref, delta_ref) = refs[:-2], refs[-2:]
    shard = lax.axis_index("seq")
    delta = (total_ref[...] + head_sum(LAST, weight_ref, blocks)) * gate_ref[:, :1]
    for i in range(NSEQ):
        delta_ref[i] = delta[BLOCK * i : BLOCK * (i + 1)]
    for s in range(NSEQ):
        first = table_ref[0, s]
        counter = lax.rem(shard + NSEQ * NSEQ - first, NSEQ)
        for half in range(2):
            place = jnp.minimum((first + counter) // NSEQ + half, NSEQ - 1)
            out_ref[s, half] = delta_ref[place].astype(BF16)


def blend_kernel(table_ref, hot_ref, rows_ref, back_ref, out_hbm, update_ref, out_ref, sems):
    first = table_ref[0, lax.axis_index("seq")]
    for j in range(0, SLOTS // BLOCK, 2):
        pair = [
            back_ref[lax.rem(first + k, NSEQ), k // NSEQ].astype(F32) for k in (j, j + 1)
        ]
        update_ref[BLOCK * j : BLOCK * (j + 2)] = jnp.concatenate(pair, axis=0).astype(BF16)
    parts = out_ref.shape[0]
    wide = SRC // parts
    copies = []
    for p in range(parts):
        here = slice(wide * p, wide * (p + 1))
        added = jnp.dot(hot_ref[here], update_ref[...], preferred_element_type=F32)
        out_ref[p] = (rows_ref[here].astype(F32) + added).astype(BF16)
        copies.append(pltpu.make_async_copy(out_ref.at[p], out_hbm.at[pl.ds(wide * p, wide), :], sems.at[p]))
        copies[p].start()
    for copy in copies:
        copy.wait()


def z_step(array, steps):
    pairs = [(z * 2 + c, (z + steps) % 4 * 2 + c) for z in range(4) for c in range(2)]
    return lax.ppermute(array, "mp", pairs)


def other_core(array):
    return lax.ppermute(array, "mp", [(m, m ^ 1) for m in range(NMP)])


def hand_on_kernel(in_ref, token_ref, out_ref):
    out_ref[...] = in_ref[...]


def hand_on(array, token):
    return pl.pallas_call(
        hand_on_kernel,
        out_shape=pltpu.VMEM(array.shape, array.dtype),
        in_specs=[VMEM, ANY],
        out_specs=VMEM,
        compiler_params=params(4),
        name="hand_on",
    )(array, token)


def z_blocks(array):
    return {0: array, 2: z_step(array, 1), 6: z_step(array, 3), 4: z_step(array, 2)}


def add_cores(blocks, token):
    for k in (6, 2, 4):
        blocks[k + 1] = other_core(hand_on(blocks[k], token) if k == 6 else blocks[k])


def shape(dims, dtype=BF16):
    return jax.ShapeDtypeStruct(dims, dtype)


def on_device(
    residual_activations,
    prelayer_gain_vector,
    gating_projection,
    asker_projection,
    lookup_projection,
    content_projection,
    final_projection,
    logit_sharpness,
    selection_table,
    dispatched_tally_table,
):
    outgoing, table, sharpness = pl.pallas_call(
        pick_kernel,
        out_shape=(
            pltpu.VMEM((NSEQ, 2, BLOCK, FEAT), BF16),
            pltpu.SMEM((3, NSEQ), jnp.int32),
            pltpu.SMEM((GROUP,), F32),
        ),
        in_specs=[HBM] * 4,
        out_specs=(VMEM, SMEM, SMEM),
        scratch_shapes=[
            pltpu.VMEM((3, NSEQ), jnp.int32),
            pltpu.VMEM((NSEQ, NSEQ), jnp.int32),
            pltpu.VMEM((1, SLOTS), jnp.int32),
            pltpu.VMEM((4, SRC // 4, FEAT), BF16),
            pltpu.SemaphoreType.DMA((8,)),
        ],
        compiler_params=params(16),
        name="pick",
    )(
        in_hbm(dispatched_tally_table),
        in_hbm(selection_table),
        in_hbm(residual_activations),
        in_hbm(logit_sharpness),
    )
    incoming = lax.all_to_all(outgoing, "seq", split_axis=0, concat_axis=0, tiled=True)
    tokens = pl.pallas_call(
        compact_kernel,
        out_shape=shape((OWNED, FEAT)),
        in_specs=[SMEM, VMEM],
        out_specs=VMEM,
        compiler_params=params(4),
        name="compact",
    )(table, incoming)
    lookup, content, asker, loaded = pl.pallas_call(
        load_in_kernel,
        out_shape=(
            pltpu.VMEM((WIDTH, HEAD), BF16),
            pltpu.VMEM((WIDTH, HEAD), BF16),
            pltpu.VMEM((WIDTH, GROUP * HEAD), BF16),
            pltpu.VMEM((8, 128), F32),
        ),
        in_specs=[HBM] * 3 + [ANY],
        out_specs=[VMEM] * 4,
        scratch_shapes=[pltpu.SemaphoreType.DMA((12,))],
        compiler_params=params(8),
        name="load_in",
    )(in_hbm(lookup_projection), in_hbm(content_projection), in_hbm(asker_projection), tokens)
    blocks = z_blocks(tokens)
    blocks[1] = other_core(tokens)
    add_cores(blocks, loaded)
    blocks = [blocks[k] for k in range(NMP)]
    query, pair = pl.pallas_call(
        project_in_kernel,
        out_shape=(
            pltpu.VMEM((OWNED, GROUP * HEAD), BF16),
            pltpu.VMEM((NSEQ, OWNED, 2 * HEAD), BF16),
        ),
        in_specs=[VMEM] * (4 + NMP),
        out_specs=[VMEM] * 2,
        scratch_shapes=[pltpu.VMEM((NMP, FEAT // 128, 128), F32)],
        compiler_params=params(16),
        cost_estimate=cost(2 * OWNED * WIDTH * 10 * HEAD, 4 * MIB),
        name="project_in",
    )(
        prelayer_gain_vector.reshape(WIDTH // 128, 128),
        asker,
        lookup,
        content,
        *blocks,
    )
    pairs = lax.all_to_all(pair, "seq", split_axis=0, concat_axis=0, tiled=True)

    attended = pl.pallas_call(
        attention_kernel,
        out_shape=shape((OWNED, GROUP * HEAD)),
        in_specs=[SMEM, VMEM, VMEM],
        out_specs=VMEM,
        compiler_params=params(24),
        name="attend",
    )(sharpness, query, pairs)
    final, total, gate, hot = pl.pallas_call(
        load_out_kernel,
        out_shape=(
            pltpu.VMEM((NMP * GROUP * HEAD, FEAT), BF16),
            pltpu.VMEM((OWNED, FEAT), F32),
            pltpu.VMEM((OWNED, 128), F32),
            pltpu.VMEM((SRC, SLOTS), BF16),
        ),
        in_specs=[HBM] + [VMEM] * (4 + NMP),
        out_specs=[VMEM] * 4,
        scratch_shapes=[pltpu.VMEM((NMP, FEAT // 128, 128), F32), pltpu.SemaphoreType.DMA((8,))],
        compiler_params=params(8),
        name="load_out",
    )(
        in_hbm(final_projection),
        dispatched_tally_table,
        selection_table,
        gating_projection.reshape(WIDTH // 128, 128),
        attended,
        *blocks,
    )
    heads = z_blocks(attended)
    heads[1] = other_core(attended)
    add_cores(heads, total)
    total = pl.pallas_call(
        project_middle_kernel,
        out_shape=pltpu.VMEM((OWNED, FEAT), F32),
        in_specs=[VMEM] * (2 + len(MIDDLE)),
        out_specs=VMEM,
        compiler_params=params(16),
        name="project_middle",
    )(total, final, *(heads[k] for k in MIDDLE))
    outgoing_back = pl.pallas_call(
        project_last_kernel,
        out_shape=pltpu.VMEM((NSEQ, 2, BLOCK, FEAT), BF16),
        in_specs=[SMEM] + [VMEM] * (3 + len(LAST)),
        out_specs=VMEM,
        scratch_shapes=[pltpu.VMEM((NSEQ, BLOCK, FEAT), F32)],
        compiler_params=params(16),
        name="project_last",
    )(table, gate, total, final, *(heads[k] for k in LAST))
    back = lax.all_to_all(outgoing_back, "seq", split_axis=0, concat_axis=0, tiled=True)
    return pl.pallas_call(
        blend_kernel,
        out_shape=shape((SRC, FEAT)),
        in_specs=[SMEM] + [VMEM] * 3,
        out_specs=HBM,
        scratch_shapes=[
            pltpu.VMEM((SLOTS, FEAT), BF16),
            pltpu.VMEM((4, SRC // 4, FEAT), BF16),
            pltpu.SemaphoreType.DMA((4,)),
        ],
        compiler_params=params(16),
        name="blend",
    )(table, hot, residual_activations, back)


def solution(mesh):
    placed = (
        P("seq", "mp"),
        P(),
        P(),
        P(None, "mp"),
        P(None, "mp"),
        P(None, "mp"),
        P(None, "mp"),
        P("mp"),
        P("seq", None),
        P(),
    )
    return jax.shard_map(
        on_device, mesh=mesh, in_specs=placed, out_specs=P("seq", "mp"), check_vma=False
    )
```

```python
import functools
import math

import jax
import jax.numpy as jnp
from jax import lax
from jax.experimental import pallas as pl
from jax.experimental.pallas import tpu as pltpu
from jax.sharding import PartitionSpec as P

NSEQ = 16
NMP = 8
BLOCK = 8
OWNED = 128
SLOTS = 256
SRC = 1024
FEAT = 512
WIDTH = 4096
HEAD = 128
GROUP = 8
MIB = 1 << 20

VMEM = pl.BlockSpec(memory_space=pltpu.VMEM)
SMEM = pl.BlockSpec(memory_space=pltpu.SMEM)
HBM = pl.BlockSpec(memory_space=pltpu.HBM)
ANY = pl.BlockSpec(memory_space=pl.ANY)
F32 = jnp.float32
BF16 = jnp.bfloat16


def params(mib):
    return pltpu.CompilerParams(vmem_limit_bytes=mib * MIB)


def cost(flops, bytes_accessed, transcendentals=0):
    return pl.CostEstimate(flops=flops, bytes_accessed=bytes_accessed, transcendentals=transcendentals)


def own_span(tally, shard):
    row = lax.broadcasted_iota(jnp.int32, (NSEQ, NSEQ), 0)
    before = jnp.sum(jnp.where(row < shard, tally, 0))
    mine = jnp.sum(jnp.where(row == shard, tally, 0))
    return before // BLOCK, mine


def deal(tally, shard):
    row = lax.broadcasted_iota(jnp.int32, (NSEQ, NSEQ), 0)
    lane = lax.broadcasted_iota(jnp.int32, (NSEQ, NSEQ), 1)
    total = jnp.right_shift(jnp.sum(tally, axis=1, keepdims=True), 3)
    across = jnp.sum(jnp.where(row == lane, total, 0), axis=0, keepdims=True)
    start = jnp.sum(jnp.where(lane < row, across, 0), axis=1, keepdims=True)
    start_across = jnp.sum(jnp.where(row < lane, total, 0), axis=0, keepdims=True)
    block = lane[:1] * NSEQ + shard
    past = start <= block
    source = jnp.sum(past.astype(jnp.int32), axis=0, keepdims=True) - 1
    begin = jnp.max(jnp.where(past, start, 0), axis=0, keepdims=True)
    return jnp.concatenate([start_across, source, jnp.right_shift(block - begin, 4)], axis=0)


def pick_kernel(
    tally_hbm, select_hbm, rows_hbm, sharp_hbm, out_ref, table_out, sharp_out, table_ref, tally_ref, select_ref, rows_ref, sems
):
    parts = rows_ref.shape[0]
    wide = SRC // parts
    copies = [
        pltpu.make_async_copy(tally_hbm, tally_ref, sems.at[parts]),
        pltpu.make_async_copy(select_hbm, select_ref, sems.at[parts + 1]),
    ] + [
        pltpu.make_async_copy(rows_hbm.at[pl.ds(wide * p, wide), :], rows_ref.at[p], sems.at[p])
        for p in range(parts)
    ]
    copies.append(pltpu.make_async_copy(sharp_hbm, sharp_out, sems.at[parts + 3]))
    for copy in copies:
        copy.start()
    copies[0].wait()
    copies[1].wait()
    tally = tally_ref[...]
    shard = lax.axis_index("seq")
    first, count = own_span(tally, shard)
    table_ref[...] = deal(tally, shard)
    dealt = pltpu.make_async_copy(table_ref, table_out, sems.at[parts + 2])
    dealt.start()
    listed = select_ref[...]
    slot = lax.broadcasted_iota(jnp.int32, (1, SLOTS), 1)
    listed = jnp.where(slot < count, listed, -1).astype(F32)
    column = jnp.broadcast_to(listed, (128, SLOTS)).T
    lane = lax.broadcasted_iota(jnp.int32, (SLOTS, 128), 1).astype(F32)
    picked = jnp.zeros((SLOTS, FEAT), F32)
    for p in range(parts):
        hot = jnp.concatenate(
            [(column == lane + float(wide * p + 128 * k)).astype(F32) for k in range(wide // 128)],
            axis=1,
        ).astype(BF16)
        copies[2 + p].wait()
        picked = picked + jnp.dot(hot, rows_ref[p], preferred_element_type=F32)
    for j in range(SLOTS // BLOCK):
        owner = lax.rem(first + j, NSEQ)
        out_ref[owner, j // NSEQ] = picked[BLOCK * j : BLOCK * (j + 1)].astype(BF16)
    dealt.wait()
    copies[-1].wait()


def in_hbm(array):
    return pltpu.with_memory_space_constraint(array, pltpu.HBM)


def block_rows(k, wide):
    return pl.ds(pl.multiple_of(block_of(k) * wide, wide), wide)


def fetch(source, target, sems, first, parts):
    wide = source.shape[0] // parts
    copies = [
        pltpu.make_async_copy(
            source.at[pl.ds(wide * p, wide), :], target.at[pl.ds(wide * p, wide), :], sems.at[first + p]
        )
        for p in range(parts)
    ]
    for copy in copies:
        copy.start()
    return copies


def load_in_kernel(keys_hbm, values_hbm, query_hbm, after_ref, keys_ref, values_ref, query_ref, done_ref, sems):
    copies = fetch(keys_hbm, keys_ref, sems, 0, 2)
    copies += fetch(values_hbm, values_ref, sems, 2, 2)
    copies += fetch(query_hbm, query_ref, sems, 4, 8)
    done_ref[...] = jnp.zeros_like(done_ref)
    for copy in copies:
        copy.wait()


def compact_kernel(table_ref, in_ref, out_ref):
    for i in range(0, NSEQ, 2):
        pair = [
            in_ref[table_ref[1, k], table_ref[2, k]].astype(F32) for k in (i, i + 1)
        ]
        out_ref[BLOCK * i : BLOCK * (i + 2)] = jnp.concatenate(pair, axis=0).astype(BF16)


def block_of(k):
    me = lax.axis_index("mp")
    chip = lax.rem(me // 2 + (4 - k // 2), 4)
    core = lax.rem(lax.rem(me, 2) + k % 2, 2)
    return chip * 2 + core


def spread(packed_ref, spread_ref):
    wide = packed_ref[...].astype(F32)
    parts = FEAT // 128
    for r in range(WIDTH // 128):
        spread_ref[r // parts, r % parts : r % parts + 1] = wide[r : r + 1]


def project_in_kernel(gain_in, query_weight_ref, keys_ref, values_ref, *refs):
    blocks, (query_ref, pair_ref, gain_ref) = refs[:NMP], refs[NMP:]
    parts = FEAT // 128
    spread(gain_in, gain_ref)
    squares = jnp.zeros((OWNED, 128), F32)
    for k in range(NMP):
        for c in range(parts):
            wide = blocks[k][:, 128 * c : 128 * (c + 1)].astype(F32)
            squares = squares + wide * wide
    inverse = lax.rsqrt(jnp.sum(squares, axis=1, keepdims=True) / WIDTH + 1e-05)
    query = jnp.zeros((OWNED, GROUP * HEAD), F32)
    keys = jnp.zeros((OWNED, HEAD), F32)
    values = jnp.zeros((OWNED, HEAD), F32)
    for k in range(NMP):
        m = block_of(k)
        rows = block_rows(k, FEAT)
        gain = gain_ref[m]
        normed = jnp.concatenate(
            [
                (
                    blocks[k][:, 128 * c : 128 * (c + 1)].astype(F32) * inverse * gain[c : c + 1]
                ).astype(BF16)
                for c in range(parts)
            ],
            axis=1,
        )
        keys = keys + jnp.dot(normed, keys_ref[rows, :], preferred_element_type=F32)
        values = values + jnp.dot(normed, values_ref[rows, :], preferred_element_type=F32)
        query = query + jnp.dot(normed, query_weight_ref[rows, :], preferred_element_type=F32)
    query_ref[...] = query.astype(BF16)
    keys = keys.astype(BF16)
    values = values.astype(BF16)
    for d in range(NSEQ):
        pair_ref[d, :, :HEAD] = keys
        pair_ref[d, :, HEAD:] = values


def attention_kernel(sharp_ref, query_ref, pair_ref, out_ref):
    shard = lax.axis_index("seq")
    step = 4 * BLOCK
    rows = GROUP * step
    many = NSEQ * step
    scale = jnp.concatenate(
        [
            jnp.full((step, 1), sharp_ref[h] * (math.log2(math.e) / math.sqrt(HEAD)), F32)
            for h in range(GROUP)
        ],
        axis=0,
    )
    q_row = lax.rem(lax.broadcasted_iota(jnp.int32, (rows, 1), 0), step)
    q_place = (q_row // BLOCK * NSEQ + shard) * BLOCK + q_row % BLOCK
    k_row = lax.broadcasted_iota(jnp.int32, (1, many), 1)
    k_place = ((k_row % step) // BLOCK * NSEQ + k_row // step) * BLOCK + k_row % BLOCK
    allowed = k_place <= q_place

    def scores_of(j):
        query = jnp.concatenate(
            [query_ref[step * j : step * (j + 1), HEAD * h : HEAD * (h + 1)] for h in range(GROUP)],
            axis=0,
        )
        scores = []
        for c in range(j + 1):
            keys = pair_ref[:, step * c : step * (c + 1), :HEAD].reshape(many, HEAD)
            score = lax.dot_general(
                query, keys, (((1,), (1,)), ((), ())), preferred_element_type=F32
            )
            scores.append(jnp.where(allowed, score, -1e30) if c == j else score)
        return scores

    later = scores_of(3)
    for j in (3, 2, 1, 0):
        scores = later
        if j:
            later = scores_of(j - 1)
        best = functools.reduce(
            jnp.maximum, [jnp.max(score, axis=1, keepdims=True) for score in scores]
        )
        offset = best * scale
        total = jnp.zeros((rows, 1), F32)
        mixed = jnp.zeros((rows, HEAD), F32)
        for c, score in enumerate(scores):
            weight = jnp.exp2(score * scale - offset)
            total = total + jnp.sum(weight, axis=1, keepdims=True)
            values = pair_ref[:, step * c : step * (c + 1), HEAD:].reshape(many, HEAD)
            mixed = mixed + jnp.dot(weight.astype(BF16), values, preferred_element_type=F32)
        mixed = (mixed / total).astype(BF16)
        for h in range(GROUP):
            out_ref[step * j : step * (j + 1), HEAD * h : HEAD * (h + 1)] = mixed[
                step * h : step * (h + 1)
            ]


MIDDLE, LAST = (1, 2, 4, 5, 6), (3, 7)


def head_sum(which, weight_ref, blocks):
    wide = GROUP * HEAD
    total = jnp.zeros((OWNED, FEAT), F32)
    for k, block in zip(which, blocks):
        total = total + jnp.dot(
            block[...], weight_ref[block_rows(k, wide), :], preferred_element_type=F32
        )
    return total


def load_out_kernel(weight_hbm, tally_ref, select_ref, gate_in, own_ref, *refs):
    tokens, (weight_ref, total_ref, gate_ref, hot_ref, gate_weight_ref, sems) = refs[:NMP], refs[NMP:]
    copies = fetch(weight_hbm, weight_ref, sems, 0, 8)
    spread(gate_in, gate_weight_ref)
    routed = jnp.zeros((OWNED, 128), F32)
    for k in range(NMP):
        weights = gate_weight_ref[block_of(k)]
        for c in range(FEAT // 128):
            routed = routed + tokens[k][:, 128 * c : 128 * (c + 1)].astype(F32) * weights[c : c + 1]
    gate_ref[...] = jnp.broadcast_to(
        jax.nn.sigmoid(jnp.sum(routed, axis=1, keepdims=True)), (OWNED, 128)
    )
    first, count = own_span(tally_ref[...], lax.axis_index("seq"))
    slot = lax.broadcasted_iota(jnp.int32, (1, SLOTS), 1)
    listed = jnp.where(slot < count, select_ref[...], -1)
    token = lax.broadcasted_iota(jnp.int32, (SRC, 1), 0)
    hot_ref[...] = (listed == token).astype(F32).astype(BF16)
    for copy in copies:
        copy.wait()
    total_ref[...] = head_sum((0,), weight_ref, (own_ref,))


def project_middle_kernel(total_in, weight_ref, *refs):
    refs[-1][...] = total_in[...] + head_sum(MIDDLE, weight_ref, refs[:-1])


def project_last_kernel(table_ref, gate_ref, total_ref, weight_ref, *refs):
    blocks, (out_ref, delta_ref) = refs[:-2], refs[-2:]
    shard = lax.axis_index("seq")
    delta = (total_ref[...] + head_sum(LAST, weight_ref, blocks)) * gate_ref[:, :1]
    for i in range(NSEQ):
        delta_ref[i] = delta[BLOCK * i : BLOCK * (i + 1)]
    for s in range(NSEQ):
        first = table_ref[0, s]
        counter = lax.rem(shard + NSEQ * NSEQ - first, NSEQ)
        for half in range(2):
            place = jnp.minimum((first + counter) // NSEQ + half, NSEQ - 1)
            out_ref[s, half] = delta_ref[place].astype(BF16)


def blend_kernel(table_ref, hot_ref, rows_ref, back_ref, out_hbm, update_ref, out_ref, sems):
    first = table_ref[0, lax.axis_index("seq")]
    for j in range(0, SLOTS // BLOCK, 2):
        pair = [
            back_ref[lax.rem(first + k, NSEQ), k // NSEQ].astype(F32) for k in (j, j + 1)
        ]
        update_ref[BLOCK * j : BLOCK * (j + 2)] = jnp.concatenate(pair, axis=0).astype(BF16)
    parts = out_ref.shape[0]
    wide = SRC // parts
    copies = []
    for p in range(parts):
        here = slice(wide * p, wide * (p + 1))
        added = jnp.dot(hot_ref[here], update_ref[...], preferred_element_type=F32)
        out_ref[p] = (rows_ref[here].astype(F32) + added).astype(BF16)
        copies.append(pltpu.make_async_copy(out_ref.at[p], out_hbm.at[pl.ds(wide * p, wide), :], sems.at[p]))
        copies[p].start()
    for copy in copies:
        copy.wait()


def z_step(array, steps):
    pairs = [(z * 2 + c, (z + steps) % 4 * 2 + c) for z in range(4) for c in range(2)]
    return lax.ppermute(array, "mp", pairs)


def other_core(array):
    return lax.ppermute(array, "mp", [(m, m ^ 1) for m in range(NMP)])


def hand_on_kernel(in_ref, token_ref, out_ref):
    out_ref[...] = in_ref[...]


def hand_on(array, token):
    return pl.pallas_call(
        hand_on_kernel,
        out_shape=pltpu.VMEM(array.shape, array.dtype),
        in_specs=[VMEM, ANY],
        out_specs=VMEM,
        compiler_params=params(4),
        name="hand_on",
    )(array, token)


def z_blocks(array):
    return {0: array, 2: z_step(array, 1), 6: z_step(array, 3), 4: z_step(array, 2)}


def add_cores(blocks, token):
    for k in (6, 2, 4):
        blocks[k + 1] = other_core(hand_on(blocks[k], token) if k == 6 else blocks[k])


def shape(dims, dtype=BF16):
    return jax.ShapeDtypeStruct(dims, dtype)


def on_device(
    residual_activations,
    prelayer_gain_vector,
    gating_projection,
    asker_projection,
    lookup_projection,
    content_projection,
    final_projection,
    logit_sharpness,
    selection_table,
    dispatched_tally_table,
):
    outgoing, table, sharpness = pl.pallas_call(
        pick_kernel,
        out_shape=(
            pltpu.VMEM((NSEQ, 2, BLOCK, FEAT), BF16),
            pltpu.SMEM((3, NSEQ), jnp.int32),
            pltpu.SMEM((GROUP,), F32),
        ),
        in_specs=[HBM] * 4,
        out_specs=(VMEM, SMEM, SMEM),
        scratch_shapes=[
            pltpu.VMEM((3, NSEQ), jnp.int32),
            pltpu.VMEM((NSEQ, NSEQ), jnp.int32),
            pltpu.VMEM((1, SLOTS), jnp.int32),
            pltpu.VMEM((4, SRC // 4, FEAT), BF16),
            pltpu.SemaphoreType.DMA((8,)),
        ],
        compiler_params=params(16),
        name="pick",
    )(
        in_hbm(dispatched_tally_table),
        in_hbm(selection_table),
        in_hbm(residual_activations),
        in_hbm(logit_sharpness),
    )
    incoming = lax.all_to_all(outgoing, "seq", split_axis=0, concat_axis=0, tiled=True)
    tokens = pl.pallas_call(
        compact_kernel,
        out_shape=shape((OWNED, FEAT)),
        in_specs=[SMEM, VMEM],
        out_specs=VMEM,
        compiler_params=params(4),
        name="compact",
    )(table, incoming)
    lookup, content, asker, loaded = pl.pallas_call(
        load_in_kernel,
        out_shape=(
            pltpu.VMEM((WIDTH, HEAD), BF16),
            pltpu.VMEM((WIDTH, HEAD), BF16),
            pltpu.VMEM((WIDTH, GROUP * HEAD), BF16),
            pltpu.VMEM((8, 128), F32),
        ),
        in_specs=[HBM] * 3 + [ANY],
        out_specs=[VMEM] * 4,
        scratch_shapes=[pltpu.SemaphoreType.DMA((12,))],
        compiler_params=params(8),
        name="load_in",
    )(in_hbm(lookup_projection), in_hbm(content_projection), in_hbm(asker_projection), tokens)
    blocks = z_blocks(tokens)
    blocks[1] = other_core(tokens)
    add_cores(blocks, loaded)
    blocks = [blocks[k] for k in range(NMP)]
    query, pair = pl.pallas_call(
        project_in_kernel,
        out_shape=(
            pltpu.VMEM((OWNED, GROUP * HEAD), BF16),
            pltpu.VMEM((NSEQ, OWNED, 2 * HEAD), BF16),
        ),
        in_specs=[VMEM] * (4 + NMP),
        out_specs=[VMEM] * 2,
        scratch_shapes=[pltpu.VMEM((NMP, FEAT // 128, 128), F32)],
        compiler_params=params(16),
        cost_estimate=cost(2 * OWNED * WIDTH * 10 * HEAD, 4 * MIB),
        name="project_in",
    )(
        prelayer_gain_vector.reshape(WIDTH // 128, 128),
        asker,
        lookup,
        content,
        *blocks,
    )
    pairs = lax.all_to_all(pair, "seq", split_axis=0, concat_axis=0, tiled=True)

    attended = pl.pallas_call(
        attention_kernel,
        out_shape=shape((OWNED, GROUP * HEAD)),
        in_specs=[SMEM, VMEM, VMEM],
        out_specs=VMEM,
        compiler_params=params(24),
        name="attend",
    )(sharpness, query, pairs)
    final, total, gate, hot = pl.pallas_call(
        load_out_kernel,
        out_shape=(
            pltpu.VMEM((NMP * GROUP * HEAD, FEAT), BF16),
            pltpu.VMEM((OWNED, FEAT), F32),
            pltpu.VMEM((OWNED, 128), F32),
            pltpu.VMEM((SRC, SLOTS), BF16),
        ),
        in_specs=[HBM] + [VMEM] * (4 + NMP),
        out_specs=[VMEM] * 4,
        scratch_shapes=[pltpu.VMEM((NMP, FEAT // 128, 128), F32), pltpu.SemaphoreType.DMA((8,))],
        compiler_params=params(8),
        name="load_out",
    )(
        in_hbm(final_projection),
        dispatched_tally_table,
        selection_table,
        gating_projection.reshape(WIDTH // 128, 128),
        attended,
        *blocks,
    )
    heads = z_blocks(attended)
    heads[1] = other_core(attended)
    add_cores(heads, total)
    total = pl.pallas_call(
        project_middle_kernel,
        out_shape=pltpu.VMEM((OWNED, FEAT), F32),
        in_specs=[VMEM] * (2 + len(MIDDLE)),
        out_specs=VMEM,
        compiler_params=params(16),
        name="project_middle",
    )(total, final, *(heads[k] for k in MIDDLE))
    outgoing_back = pl.pallas_call(
        project_last_kernel,
        out_shape=pltpu.VMEM((NSEQ, 2, BLOCK, FEAT), BF16),
        in_specs=[SMEM] + [VMEM] * (3 + len(LAST)),
        out_specs=VMEM,
        scratch_shapes=[pltpu.VMEM((NSEQ, BLOCK, FEAT), F32)],
        compiler_params=params(16),
        name="project_last",
    )(table, gate, total, final, *(heads[k] for k in LAST))
    back = lax.all_to_all(outgoing_back, "seq", split_axis=0, concat_axis=0, tiled=True)
    return pl.pallas_call(
        blend_kernel,
        out_shape=shape((SRC, FEAT)),
        in_specs=[SMEM] + [VMEM] * 3,
        out_specs=HBM,
        scratch_shapes=[
            pltpu.VMEM((SLOTS, FEAT), BF16),
            pltpu.VMEM((4, SRC // 4, FEAT), BF16),
            pltpu.SemaphoreType.DMA((4,)),
        ],
        compiler_params=params(16),
        name="blend",
    )(table, hot, residual_activations, back)


def solution(mesh):
    placed = (
        P("seq", "mp"),
        P(),
        P(),
        P(None, "mp"),
        P(None, "mp"),
        P(None, "mp"),
        P(None, "mp"),
        P("mp"),
        P("seq", None),
        P(),
    )
    return jax.shard_map(
        on_device, mesh=mesh, in_specs=placed, out_specs=P("seq", "mp"), check_vma=False
    )
```

```python
import functools
import math

import jax
import jax.numpy as jnp
from jax import lax
from jax.experimental import pallas as pl
from jax.experimental.pallas import tpu as pltpu
from jax.sharding import PartitionSpec as P

NSEQ = 16
NMP = 8
BLOCK = 8
OWNED = 128
SLOTS = 256
SRC = 1024
FEAT = 512
WIDTH = 4096
HEAD = 128
GROUP = 8
MIB = 1 << 20

VMEM = pl.BlockSpec(memory_space=pltpu.VMEM)
SMEM = pl.BlockSpec(memory_space=pltpu.SMEM)
HBM = pl.BlockSpec(memory_space=pltpu.HBM)
ANY = pl.BlockSpec(memory_space=pl.ANY)
F32 = jnp.float32
BF16 = jnp.bfloat16


def params(mib):
    return pltpu.CompilerParams(vmem_limit_bytes=mib * MIB)


def cost(flops, bytes_accessed, transcendentals=0):
    return pl.CostEstimate(flops=flops, bytes_accessed=bytes_accessed, transcendentals=transcendentals)


def own_span(tally, shard):
    row = lax.broadcasted_iota(jnp.int32, (NSEQ, NSEQ), 0)
    before = jnp.sum(jnp.where(row < shard, tally, 0))
    mine = jnp.sum(jnp.where(row == shard, tally, 0))
    return before // BLOCK, mine


def deal(tally, shard):
    row = lax.broadcasted_iota(jnp.int32, (NSEQ, NSEQ), 0)
    lane = lax.broadcasted_iota(jnp.int32, (NSEQ, NSEQ), 1)
    total = jnp.right_shift(jnp.sum(tally, axis=1, keepdims=True), 3)
    across = jnp.sum(jnp.where(row == lane, total, 0), axis=0, keepdims=True)
    start = jnp.sum(jnp.where(lane < row, across, 0), axis=1, keepdims=True)
    start_across = jnp.sum(jnp.where(row < lane, total, 0), axis=0, keepdims=True)
    block = lane[:1] * NSEQ + shard
    past = start <= block
    source = jnp.sum(past.astype(jnp.int32), axis=0, keepdims=True) - 1
    begin = jnp.max(jnp.where(past, start, 0), axis=0, keepdims=True)
    return jnp.concatenate([start_across, source, jnp.right_shift(block - begin, 4)], axis=0)


def pick_kernel(
    tally_hbm, select_hbm, rows_hbm, sharp_hbm, out_ref, table_out, sharp_out, table_ref, tally_ref, select_ref, rows_ref, sems
):
    parts = rows_ref.shape[0]
    wide = SRC // parts
    copies = [
        pltpu.make_async_copy(tally_hbm, tally_ref, sems.at[parts]),
        pltpu.make_async_copy(select_hbm, select_ref, sems.at[parts + 1]),
    ] + [
        pltpu.make_async_copy(rows_hbm.at[pl.ds(wide * p, wide), :], rows_ref.at[p], sems.at[p])
        for p in range(parts)
    ]
    copies.append(pltpu.make_async_copy(sharp_hbm, sharp_out, sems.at[parts + 3]))
    for copy in copies:
        copy.start()
    copies[0].wait()
    copies[1].wait()
    tally = tally_ref[...]
    shard = lax.axis_index("seq")
    first, count = own_span(tally, shard)
    table_ref[...] = deal(tally, shard)
    dealt = pltpu.make_async_copy(table_ref, table_out, sems.at[parts + 2])
    dealt.start()
    listed = select_ref[...]
    slot = lax.broadcasted_iota(jnp.int32, (1, SLOTS), 1)
    listed = jnp.where(slot < count, listed, -1).astype(F32)
    column = jnp.broadcast_to(listed, (128, SLOTS)).T
    lane = lax.broadcasted_iota(jnp.int32, (SLOTS, 128), 1).astype(F32)
    picked = jnp.zeros((SLOTS, FEAT), F32)
    for p in range(parts):
        hot = jnp.concatenate(
            [(column == lane + float(wide * p + 128 * k)).astype(F32) for k in range(wide // 128)],
            axis=1,
        ).astype(BF16)
        copies[2 + p].wait()
        picked = picked + jnp.dot(hot, rows_ref[p], preferred_element_type=F32)
    for j in range(SLOTS // BLOCK):
        owner = lax.rem(first + j, NSEQ)
        out_ref[owner, j // NSEQ] = picked[BLOCK * j : BLOCK * (j + 1)].astype(BF16)
    dealt.wait()
    copies[-1].wait()


def in_hbm(array):
    return pltpu.with_memory_space_constraint(array, pltpu.HBM)


def block_rows(k, wide):
    return pl.ds(pl.multiple_of(block_of(k) * wide, wide), wide)


def fetch(source, target, sems, first, parts):
    wide = source.shape[0] // parts
    copies = [
        pltpu.make_async_copy(
            source.at[pl.ds(wide * p, wide), :], target.at[pl.ds(wide * p, wide), :], sems.at[first + p]
        )
        for p in range(parts)
    ]
    for copy in copies:
        copy.start()
    return copies


def load_in_kernel(keys_hbm, values_hbm, query_hbm, after_ref, keys_ref, values_ref, query_ref, done_ref, sems):
    copies = fetch(keys_hbm, keys_ref, sems, 0, 2)
    copies += fetch(values_hbm, values_ref, sems, 2, 2)
    copies += fetch(query_hbm, query_ref, sems, 4, 8)
    done_ref[...] = jnp.zeros_like(done_ref)
    for copy in copies:
        copy.wait()


def compact_kernel(table_ref, in_ref, out_ref):
    for i in range(0, NSEQ, 2):
        pair = [
            in_ref[table_ref[1, k], table_ref[2, k]].astype(F32) for k in (i, i + 1)
        ]
        out_ref[BLOCK * i : BLOCK * (i + 2)] = jnp.concatenate(pair, axis=0).astype(BF16)


def block_of(k):
    me = lax.axis_index("mp")
    chip = lax.rem(me // 2 + (4 - k // 2), 4)
    core = lax.rem(lax.rem(me, 2) + k % 2, 2)
    return chip * 2 + core


def spread(packed_ref, spread_ref):
    wide = packed_ref[...].astype(F32)
    parts = FEAT // 128
    for r in range(WIDTH // 128):
        spread_ref[r // parts, r % parts : r % parts + 1] = wide[r : r + 1]


def square_sum(blocks):
    total = jnp.zeros((OWNED, 128), F32)
    for block in blocks:
        for c in range(FEAT // 128):
            wide = block[:, 128 * c : 128 * (c + 1)].astype(F32)
            total = total + wide * wide
    return total


def square_kernel(*refs):
    refs[-1][...] = square_sum(refs[:-1])


def project_in_kernel(squares_ref, gain_in, query_weight_ref, keys_ref, values_ref, *refs):
    blocks, (query_ref, pair_ref, gain_ref) = refs[:NMP], refs[NMP:]
    parts = FEAT // 128
    spread(gain_in, gain_ref)
    squares = squares_ref[...] + square_sum([blocks[k] for k in (1, 3, 5, 7)])
    inverse = lax.rsqrt(jnp.sum(squares, axis=1, keepdims=True) / WIDTH + 1e-05)
    query = jnp.zeros((OWNED, GROUP * HEAD), F32)
    keys = jnp.zeros((OWNED, HEAD), F32)
    values = jnp.zeros((OWNED, HEAD), F32)
    for k in range(NMP):
        m = block_of(k)
        rows = block_rows(k, FEAT)
        gain = gain_ref[m]
        normed = jnp.concatenate(
            [
                (
                    blocks[k][:, 128 * c : 128 * (c + 1)].astype(F32) * inverse * gain[c : c + 1]
                ).astype(BF16)
                for c in range(parts)
            ],
            axis=1,
        )
        keys = keys + jnp.dot(normed, keys_ref[rows, :], preferred_element_type=F32)
        values = values + jnp.dot(normed, values_ref[rows, :], preferred_element_type=F32)
        query = query + jnp.dot(normed, query_weight_ref[rows, :], preferred_element_type=F32)
    query_ref[...] = query.astype(BF16)
    keys = keys.astype(BF16)
    values = values.astype(BF16)
    for d in range(NSEQ):
        pair_ref[d, :, :HEAD] = keys
        pair_ref[d, :, HEAD:] = values


def attention_kernel(sharp_ref, query_ref, pair_ref, out_ref):
    shard = lax.axis_index("seq")
    step = 4 * BLOCK
    rows = GROUP * step
    many = NSEQ * step
    scale = jnp.concatenate(
        [
            jnp.full((step, 1), sharp_ref[h] * (math.log2(math.e) / math.sqrt(HEAD)), F32)
            for h in range(GROUP)
        ],
        axis=0,
    )
    q_row = lax.rem(lax.broadcasted_iota(jnp.int32, (rows, 1), 0), step)
    q_place = (q_row // BLOCK * NSEQ + shard) * BLOCK + q_row % BLOCK
    k_row = lax.broadcasted_iota(jnp.int32, (1, many), 1)
    k_place = ((k_row % step) // BLOCK * NSEQ + k_row // step) * BLOCK + k_row % BLOCK
    allowed = k_place <= q_place

    def scores_of(j):
        query = jnp.concatenate(
            [query_ref[step * j : step * (j + 1), HEAD * h : HEAD * (h + 1)] for h in range(GROUP)],
            axis=0,
        )
        scores = []
        for c in range(j + 1):
            keys = pair_ref[:, step * c : step * (c + 1), :HEAD].reshape(many, HEAD)
            score = lax.dot_general(
                query, keys, (((1,), (1,)), ((), ())), preferred_element_type=F32
            )
            scores.append(jnp.where(allowed, score, -1e30) if c == j else score)
        return scores

    later = scores_of(3)
    for j in (3, 2, 1, 0):
        scores = later
        if j:
            later = scores_of(j - 1)
        best = functools.reduce(
            jnp.maximum, [jnp.max(score, axis=1, keepdims=True) for score in scores]
        )
        offset = best * scale
        total = jnp.zeros((rows, 1), F32)
        mixed = jnp.zeros((rows, HEAD), F32)
        for c, score in enumerate(scores):
            weight = jnp.exp2(score * scale - offset)
            total = total + jnp.sum(weight, axis=1, keepdims=True)
            values = pair_ref[:, step * c : step * (c + 1), HEAD:].reshape(many, HEAD)
            mixed = mixed + jnp.dot(weight.astype(BF16), values, preferred_element_type=F32)
        mixed = (mixed / total).astype(BF16)
        for h in range(GROUP):
            out_ref[step * j : step * (j + 1), HEAD * h : HEAD * (h + 1)] = mixed[
                step * h : step * (h + 1)
            ]


MIDDLE, LAST = (1, 2, 4, 5, 6), (3, 7)


def head_sum(which, weight_ref, blocks):
    wide = GROUP * HEAD
    total = jnp.zeros((OWNED, FEAT), F32)
    for k, block in zip(which, blocks):
        total = total + jnp.dot(
            block[...], weight_ref[block_rows(k, wide), :], preferred_element_type=F32
        )
    return total


def load_out_kernel(weight_hbm, tally_ref, select_ref, gate_in, own_ref, *refs):
    tokens, (weight_ref, total_ref, gate_ref, hot_ref, gate_weight_ref, sems) = refs[:NMP], refs[NMP:]
    copies = fetch(weight_hbm, weight_ref, sems, 0, 8)
    spread(gate_in, gate_weight_ref)
    routed = jnp.zeros((OWNED, 128), F32)
    for k in range(NMP):
        weights = gate_weight_ref[block_of(k)]
        for c in range(FEAT // 128):
            routed = routed + tokens[k][:, 128 * c : 128 * (c + 1)].astype(F32) * weights[c : c + 1]
    gate_ref[...] = jnp.broadcast_to(
        jax.nn.sigmoid(jnp.sum(routed, axis=1, keepdims=True)), (OWNED, 128)
    )
    first, count = own_span(tally_ref[...], lax.axis_index("seq"))
    slot = lax.broadcasted_iota(jnp.int32, (1, SLOTS), 1)
    listed = jnp.where(slot < count, select_ref[...], -1)
    token = lax.broadcasted_iota(jnp.int32, (SRC, 1), 0)
    hot_ref[...] = (listed == token).astype(F32).astype(BF16)
    for copy in copies:
        copy.wait()
    total_ref[...] = head_sum((0,), weight_ref, (own_ref,))


def project_middle_kernel(total_in, weight_ref, *refs):
    refs[-1][...] = total_in[...] + head_sum(MIDDLE, weight_ref, refs[:-1])


def project_last_kernel(table_ref, gate_ref, total_ref, weight_ref, *refs):
    blocks, (out_ref, delta_ref) = refs[:-2], refs[-2:]
    shard = lax.axis_index("seq")
    delta = (total_ref[...] + head_sum(LAST, weight_ref, blocks)) * gate_ref[:, :1]
    for i in range(NSEQ):
        delta_ref[i] = delta[BLOCK * i : BLOCK * (i + 1)]
    for s in range(NSEQ):
        first = table_ref[0, s]
        counter = lax.rem(shard + NSEQ * NSEQ - first, NSEQ)
        for half in range(2):
            place = jnp.minimum((first + counter) // NSEQ + half, NSEQ - 1)
            out_ref[s, half] = delta_ref[place].astype(BF16)


def blend_kernel(table_ref, hot_ref, rows_ref, back_ref, out_hbm, update_ref, out_ref, sems):
    first = table_ref[0, lax.axis_index("seq")]
    for j in range(0, SLOTS // BLOCK, 2):
        pair = [
            back_ref[lax.rem(first + k, NSEQ), k // NSEQ].astype(F32) for k in (j, j + 1)
        ]
        update_ref[BLOCK * j : BLOCK * (j + 2)] = jnp.concatenate(pair, axis=0).astype(BF16)
    parts = out_ref.shape[0]
    wide = SRC // parts
    copies = []
    for p in range(parts):
        here = slice(wide * p, wide * (p + 1))
        added = jnp.dot(hot_ref[here], update_ref[...], preferred_element_type=F32)
        out_ref[p] = (rows_ref[here].astype(F32) + added).astype(BF16)
        copies.append(pltpu.make_async_copy(out_ref.at[p], out_hbm.at[pl.ds(wide * p, wide), :], sems.at[p]))
        copies[p].start()
    for copy in copies:
        copy.wait()


def z_step(array, steps):
    pairs = [(z * 2 + c, (z + steps) % 4 * 2 + c) for z in range(4) for c in range(2)]
    return lax.ppermute(array, "mp", pairs)


def other_core(array):
    return lax.ppermute(array, "mp", [(m, m ^ 1) for m in range(NMP)])


def hand_on_kernel(in_ref, token_ref, out_ref):
    out_ref[...] = in_ref[...]


def hand_on(array, token):
    return pl.pallas_call(
        hand_on_kernel,
        out_shape=pltpu.VMEM(array.shape, array.dtype),
        in_specs=[VMEM, ANY],
        out_specs=VMEM,
        compiler_params=params(4),
        name="hand_on",
    )(array, token)


def z_blocks(array):
    return {0: array, 2: z_step(array, 1), 6: z_step(array, 3), 4: z_step(array, 2)}


def add_cores(blocks, token):
    for k in (6, 2, 4):
        blocks[k + 1] = other_core(hand_on(blocks[k], token) if k == 6 else blocks[k])


def shape(dims, dtype=BF16):
    return jax.ShapeDtypeStruct(dims, dtype)


def on_device(
    residual_activations,
    prelayer_gain_vector,
    gating_projection,
    asker_projection,
    lookup_projection,
    content_projection,
    final_projection,
    logit_sharpness,
    selection_table,
    dispatched_tally_table,
):
    outgoing, table, sharpness = pl.pallas_call(
        pick_kernel,
        out_shape=(
            pltpu.VMEM((NSEQ, 2, BLOCK, FEAT), BF16),
            pltpu.SMEM((3, NSEQ), jnp.int32),
            pltpu.SMEM((GROUP,), F32),
        ),
        in_specs=[HBM] * 4,
        out_specs=(VMEM, SMEM, SMEM),
        scratch_shapes=[
            pltpu.VMEM((3, NSEQ), jnp.int32),
            pltpu.VMEM((NSEQ, NSEQ), jnp.int32),
            pltpu.VMEM((1, SLOTS), jnp.int32),
            pltpu.VMEM((4, SRC // 4, FEAT), BF16),
            pltpu.SemaphoreType.DMA((8,)),
        ],
        compiler_params=params(16),
        name="pick",
    )(
        in_hbm(dispatched_tally_table),
        in_hbm(selection_table),
        in_hbm(residual_activations),
        in_hbm(logit_sharpness),
    )
    incoming = lax.all_to_all(outgoing, "seq", split_axis=0, concat_axis=0, tiled=True)
    tokens = pl.pallas_call(
        compact_kernel,
        out_shape=shape((OWNED, FEAT)),
        in_specs=[SMEM, VMEM],
        out_specs=VMEM,
        compiler_params=params(4),
        name="compact",
    )(table, incoming)
    lookup, content, asker, loaded = pl.pallas_call(
        load_in_kernel,
        out_shape=(
            pltpu.VMEM((WIDTH, HEAD), BF16),
            pltpu.VMEM((WIDTH, HEAD), BF16),
            pltpu.VMEM((WIDTH, GROUP * HEAD), BF16),
            pltpu.VMEM((8, 128), F32),
        ),
        in_specs=[HBM] * 3 + [ANY],
        out_specs=[VMEM] * 4,
        scratch_shapes=[pltpu.SemaphoreType.DMA((12,))],
        compiler_params=params(8),
        name="load_in",
    )(in_hbm(lookup_projection), in_hbm(content_projection), in_hbm(asker_projection), tokens)
    blocks = z_blocks(tokens)
    blocks[1] = other_core(tokens)
    add_cores(blocks, loaded)
    blocks = [blocks[k] for k in range(NMP)]
    squares = pl.pallas_call(
        square_kernel,
        out_shape=pltpu.VMEM((OWNED, 128), F32),
        in_specs=[VMEM] * 4,
        out_specs=VMEM,
        compiler_params=params(4),
        name="square",
    )(*(blocks[k] for k in (0, 2, 4, 6)))
    query, pair = pl.pallas_call(
        project_in_kernel,
        out_shape=(
            pltpu.VMEM((OWNED, GROUP * HEAD), BF16),
            pltpu.VMEM((NSEQ, OWNED, 2 * HEAD), BF16),
        ),
        in_specs=[VMEM] * (5 + NMP),
        out_specs=[VMEM] * 2,
        scratch_shapes=[pltpu.VMEM((NMP, FEAT // 128, 128), F32)],
        compiler_params=params(16),
        cost_estimate=cost(2 * OWNED * WIDTH * 10 * HEAD, 4 * MIB),
        name="project_in",
    )(
        squares,
        prelayer_gain_vector.reshape(WIDTH // 128, 128),
        asker,
        lookup,
        content,
        *blocks,
    )
    pairs = lax.all_to_all(pair, "seq", split_axis=0, concat_axis=0, tiled=True)

    attended = pl.pallas_call(
        attention_kernel,
        out_shape=shape((OWNED, GROUP * HEAD)),
        in_specs=[SMEM, VMEM, VMEM],
        out_specs=VMEM,
        compiler_params=params(24),
        name="attend",
    )(sharpness, query, pairs)
    final, total, gate, hot = pl.pallas_call(
        load_out_kernel,
        out_shape=(
            pltpu.VMEM((NMP * GROUP * HEAD, FEAT), BF16),
            pltpu.VMEM((OWNED, FEAT), F32),
            pltpu.VMEM((OWNED, 128), F32),
            pltpu.VMEM((SRC, SLOTS), BF16),
        ),
        in_specs=[HBM] + [VMEM] * (4 + NMP),
        out_specs=[VMEM] * 4,
        scratch_shapes=[pltpu.VMEM((NMP, FEAT // 128, 128), F32), pltpu.SemaphoreType.DMA((8,))],
        compiler_params=params(8),
        name="load_out",
    )(
        in_hbm(final_projection),
        dispatched_tally_table,
        selection_table,
        gating_projection.reshape(WIDTH // 128, 128),
        attended,
        *blocks,
    )
    heads = z_blocks(attended)
    heads[1] = other_core(attended)
    add_cores(heads, total)
    total = pl.pallas_call(
        project_middle_kernel,
        out_shape=pltpu.VMEM((OWNED, FEAT), F32),
        in_specs=[VMEM] * (2 + len(MIDDLE)),
        out_specs=VMEM,
        compiler_params=params(16),
        name="project_middle",
    )(total, final, *(heads[k] for k in MIDDLE))
    outgoing_back = pl.pallas_call(
        project_last_kernel,
        out_shape=pltpu.VMEM((NSEQ, 2, BLOCK, FEAT), BF16),
        in_specs=[SMEM] + [VMEM] * (3 + len(LAST)),
        out_specs=VMEM,
        scratch_shapes=[pltpu.VMEM((NSEQ, BLOCK, FEAT), F32)],
        compiler_params=params(16),
        name="project_last",
    )(table, gate, total, final, *(heads[k] for k in LAST))
    back = lax.all_to_all(outgoing_back, "seq", split_axis=0, concat_axis=0, tiled=True)
    return pl.pallas_call(
        blend_kernel,
        out_shape=shape((SRC, FEAT)),
        in_specs=[SMEM] + [VMEM] * 3,
        out_specs=HBM,
        scratch_shapes=[
            pltpu.VMEM((SLOTS, FEAT), BF16),
            pltpu.VMEM((4, SRC // 4, FEAT), BF16),
            pltpu.SemaphoreType.DMA((4,)),
        ],
        compiler_params=params(16),
        name="blend",
    )(table, hot, residual_activations, back)


def solution(mesh):
    placed = (
        P("seq", "mp"),
        P(),
        P(),
        P(None, "mp"),
        P(None, "mp"),
        P(None, "mp"),
        P(None, "mp"),
        P("mp"),
        P("seq", None),
        P(),
    )
    return jax.shard_map(
        on_device, mesh=mesh, in_specs=placed, out_specs=P("seq", "mp"), check_vma=False
    )
```

```python
import functools
import math

import jax
import jax.numpy as jnp
from jax import lax
from jax.experimental import pallas as pl
from jax.experimental.pallas import tpu as pltpu
from jax.sharding import PartitionSpec as P

NSEQ = 16
NMP = 8
BLOCK = 8
OWNED = 128
SLOTS = 256
SRC = 1024
FEAT = 512
WIDTH = 4096
HEAD = 128
GROUP = 8
MIB = 1 << 20

VMEM = pl.BlockSpec(memory_space=pltpu.VMEM)
SMEM = pl.BlockSpec(memory_space=pltpu.SMEM)
HBM = pl.BlockSpec(memory_space=pltpu.HBM)
ANY = pl.BlockSpec(memory_space=pl.ANY)
F32 = jnp.float32
BF16 = jnp.bfloat16


def params(mib):
    return pltpu.CompilerParams(vmem_limit_bytes=mib * MIB)


def cost(flops, bytes_accessed, transcendentals=0):
    return pl.CostEstimate(flops=flops, bytes_accessed=bytes_accessed, transcendentals=transcendentals)


def own_span(tally, shard):
    row = lax.broadcasted_iota(jnp.int32, (NSEQ, NSEQ), 0)
    before = jnp.sum(jnp.where(row < shard, tally, 0))
    mine = jnp.sum(jnp.where(row == shard, tally, 0))
    return before // BLOCK, mine


def deal(tally, shard):
    row = lax.broadcasted_iota(jnp.int32, (NSEQ, NSEQ), 0)
    lane = lax.broadcasted_iota(jnp.int32, (NSEQ, NSEQ), 1)
    total = jnp.right_shift(jnp.sum(tally, axis=1, keepdims=True), 3)
    across = jnp.sum(jnp.where(row == lane, total, 0), axis=0, keepdims=True)
    start = jnp.sum(jnp.where(lane < row, across, 0), axis=1, keepdims=True)
    start_across = jnp.sum(jnp.where(row < lane, total, 0), axis=0, keepdims=True)
    block = lane[:1] * NSEQ + shard
    past = start <= block
    source = jnp.sum(past.astype(jnp.int32), axis=0, keepdims=True) - 1
    begin = jnp.max(jnp.where(past, start, 0), axis=0, keepdims=True)
    return jnp.concatenate([start_across, source, jnp.right_shift(block - begin, 4)], axis=0)


def pick_kernel(
    tally_hbm, select_hbm, rows_hbm, sharp_hbm, out_ref, table_out, sharp_out, table_ref, tally_ref, select_ref, rows_ref, sems
):
    parts = rows_ref.shape[0]
    wide = SRC // parts
    copies = [
        pltpu.make_async_copy(tally_hbm, tally_ref, sems.at[parts]),
        pltpu.make_async_copy(select_hbm, select_ref, sems.at[parts + 1]),
    ] + [
        pltpu.make_async_copy(rows_hbm.at[pl.ds(wide * p, wide), :], rows_ref.at[p], sems.at[p])
        for p in range(parts)
    ]
    copies.append(pltpu.make_async_copy(sharp_hbm, sharp_out, sems.at[parts + 3]))
    for copy in copies:
        copy.start()
    copies[0].wait()
    copies[1].wait()
    tally = tally_ref[...]
    shard = lax.axis_index("seq")
    first, count = own_span(tally, shard)
    table_ref[...] = deal(tally, shard)
    dealt = pltpu.make_async_copy(table_ref, table_out, sems.at[parts + 2])
    dealt.start()
    listed = select_ref[...]
    slot = lax.broadcasted_iota(jnp.int32, (1, SLOTS), 1)
    listed = jnp.where(slot < count, listed, -1).astype(F32)
    column = jnp.broadcast_to(listed, (128, SLOTS)).T
    lane = lax.broadcasted_iota(jnp.int32, (SLOTS, 128), 1).astype(F32)
    picked = jnp.zeros((SLOTS, FEAT), F32)
    for p in range(parts):
        hot = jnp.concatenate(
            [(column == lane + float(wide * p + 128 * k)).astype(F32) for k in range(wide // 128)],
            axis=1,
        ).astype(BF16)
        copies[2 + p].wait()
        picked = picked + jnp.dot(hot, rows_ref[p], preferred_element_type=F32)
    for j in range(SLOTS // BLOCK):
        owner = lax.rem(first + j, NSEQ)
        out_ref[owner, j // NSEQ] = picked[BLOCK * j : BLOCK * (j + 1)].astype(BF16)
    dealt.wait()
    copies[-1].wait()


def in_hbm(array):
    return pltpu.with_memory_space_constraint(array, pltpu.HBM)


def block_rows(k, wide):
    return pl.ds(pl.multiple_of(block_of(k) * wide, wide), wide)


def fetch(source, target, sems, first, parts):
    wide = source.shape[0] // parts
    copies = [
        pltpu.make_async_copy(
            source.at[pl.ds(wide * p, wide), :], target.at[pl.ds(wide * p, wide), :], sems.at[first + p]
        )
        for p in range(parts)
    ]
    for copy in copies:
        copy.start()
    return copies


def load_in_kernel(keys_hbm, values_hbm, query_hbm, after_ref, keys_ref, values_ref, query_ref, done_ref, sems):
    copies = fetch(keys_hbm, keys_ref, sems, 0, 2)
    copies += fetch(values_hbm, values_ref, sems, 2, 2)
    copies += fetch(query_hbm, query_ref, sems, 4, 8)
    done_ref[...] = jnp.zeros_like(done_ref)
    for copy in copies:
        copy.wait()


def compact_kernel(table_ref, in_ref, out_ref):
    for i in range(0, NSEQ, 2):
        pair = [
            in_ref[table_ref[1, k], table_ref[2, k]].astype(F32) for k in (i, i + 1)
        ]
        out_ref[BLOCK * i : BLOCK * (i + 2)] = jnp.concatenate(pair, axis=0).astype(BF16)


def block_of(k):
    me = lax.axis_index("mp")
    chip = lax.rem(me // 2 + (4 - k // 2), 4)
    core = lax.rem(lax.rem(me, 2) + k % 2, 2)
    return chip * 2 + core


def spread(packed_ref, spread_ref):
    wide = packed_ref[...].astype(F32)
    parts = FEAT // 128
    for r in range(WIDTH // 128):
        spread_ref[r // parts, r % parts : r % parts + 1] = wide[r : r + 1]


def square_sum(blocks):
    total = jnp.zeros((OWNED, 128), F32)
    for block in blocks:
        for c in range(FEAT // 128):
            wide = block[:, 128 * c : 128 * (c + 1)].astype(F32)
            total = total + wide * wide
    return total


def square_kernel(gain_in, *refs):
    spread(gain_in, refs[-1])
    refs[-2][...] = square_sum(refs[:-2])


def project_in_kernel(squares_ref, gain_ref, query_weight_ref, keys_ref, values_ref, *refs):
    blocks, (query_ref, pair_ref) = refs[:NMP], refs[NMP:]
    parts = FEAT // 128
    squares = squares_ref[...] + square_sum([blocks[k] for k in (1, 3, 5, 7)])
    inverse = lax.rsqrt(jnp.sum(squares, axis=1, keepdims=True) / WIDTH + 1e-05)
    query = jnp.zeros((OWNED, GROUP * HEAD), F32)
    keys = jnp.zeros((OWNED, HEAD), F32)
    values = jnp.zeros((OWNED, HEAD), F32)
    for k in range(NMP):
        m = block_of(k)
        rows = block_rows(k, FEAT)
        gain = gain_ref[m]
        normed = jnp.concatenate(
            [
                (
                    blocks[k][:, 128 * c : 128 * (c + 1)].astype(F32) * inverse * gain[c : c + 1]
                ).astype(BF16)
                for c in range(parts)
            ],
            axis=1,
        )
        keys = keys + jnp.dot(normed, keys_ref[rows, :], preferred_element_type=F32)
        values = values + jnp.dot(normed, values_ref[rows, :], preferred_element_type=F32)
        query = query + jnp.dot(normed, query_weight_ref[rows, :], preferred_element_type=F32)
    query_ref[...] = query.astype(BF16)
    keys = keys.astype(BF16)
    values = values.astype(BF16)
    for d in range(NSEQ):
        pair_ref[d, :, :HEAD] = keys
        pair_ref[d, :, HEAD:] = values


def attention_kernel(sharp_ref, query_ref, pair_ref, out_ref):
    shard = lax.axis_index("seq")
    step = 4 * BLOCK
    rows = GROUP * step
    many = NSEQ * step
    scale = jnp.concatenate(
        [
            jnp.full((step, 1), sharp_ref[h] * (math.log2(math.e) / math.sqrt(HEAD)), F32)
            for h in range(GROUP)
        ],
        axis=0,
    )
    q_row = lax.rem(lax.broadcasted_iota(jnp.int32, (rows, 1), 0), step)
    q_place = (q_row // BLOCK * NSEQ + shard) * BLOCK + q_row % BLOCK
    k_row = lax.broadcasted_iota(jnp.int32, (1, many), 1)
    k_place = ((k_row % step) // BLOCK * NSEQ + k_row // step) * BLOCK + k_row % BLOCK
    allowed = k_place <= q_place

    def scores_of(j):
        query = jnp.concatenate(
            [query_ref[step * j : step * (j + 1), HEAD * h : HEAD * (h + 1)] for h in range(GROUP)],
            axis=0,
        )
        scores = []
        for c in range(j + 1):
            keys = pair_ref[:, step * c : step * (c + 1), :HEAD].reshape(many, HEAD)
            score = lax.dot_general(
                query, keys, (((1,), (1,)), ((), ())), preferred_element_type=F32
            )
            scores.append(jnp.where(allowed, score, -1e30) if c == j else score)
        return scores

    later = scores_of(3)
    for j in (3, 2, 1, 0):
        scores = later
        if j:
            later = scores_of(j - 1)
        best = functools.reduce(
            jnp.maximum, [jnp.max(score, axis=1, keepdims=True) for score in scores]
        )
        offset = best * scale
        total = jnp.zeros((rows, 1), F32)
        mixed = jnp.zeros((rows, HEAD), F32)
        for c, score in enumerate(scores):
            weight = jnp.exp2(score * scale - offset)
            total = total + jnp.sum(weight, axis=1, keepdims=True)
            values = pair_ref[:, step * c : step * (c + 1), HEAD:].reshape(many, HEAD)
            mixed = mixed + jnp.dot(weight.astype(BF16), values, preferred_element_type=F32)
        mixed = (mixed / total).astype(BF16)
        for h in range(GROUP):
            out_ref[step * j : step * (j + 1), HEAD * h : HEAD * (h + 1)] = mixed[
                step * h : step * (h + 1)
            ]


MIDDLE, LAST = (1, 2, 4, 5, 6), (3, 7)


def head_sum(which, weight_ref, blocks):
    wide = GROUP * HEAD
    total = jnp.zeros((OWNED, FEAT), F32)
    for k, block in zip(which, blocks):
        total = total + jnp.dot(
            block[...], weight_ref[block_rows(k, wide), :], preferred_element_type=F32
        )
    return total


def load_out_kernel(weight_hbm, tally_ref, select_ref, gate_in, own_ref, *refs):
    tokens, (weight_ref, total_ref, gate_ref, hot_ref, gate_weight_ref, sems) = refs[:NMP], refs[NMP:]
    copies = fetch(weight_hbm, weight_ref, sems, 0, 8)
    spread(gate_in, gate_weight_ref)
    routed = jnp.zeros((OWNED, 128), F32)
    for k in range(NMP):
        weights = gate_weight_ref[block_of(k)]
        for c in range(FEAT // 128):
            routed = routed + tokens[k][:, 128 * c : 128 * (c + 1)].astype(F32) * weights[c : c + 1]
    gate_ref[...] = jnp.broadcast_to(
        jax.nn.sigmoid(jnp.sum(routed, axis=1, keepdims=True)), (OWNED, 128)
    )
    first, count = own_span(tally_ref[...], lax.axis_index("seq"))
    slot = lax.broadcasted_iota(jnp.int32, (1, SLOTS), 1)
    listed = jnp.where(slot < count, select_ref[...], -1)
    token = lax.broadcasted_iota(jnp.int32, (SRC, 1), 0)
    hot_ref[...] = (listed == token).astype(F32).astype(BF16)
    for copy in copies:
        copy.wait()
    total_ref[...] = head_sum((0,), weight_ref, (own_ref,))


def project_middle_kernel(total_in, weight_ref, *refs):
    refs[-1][...] = total_in[...] + head_sum(MIDDLE, weight_ref, refs[:-1])


def project_last_kernel(table_ref, gate_ref, total_ref, weight_ref, *refs):
    blocks, (out_ref, delta_ref) = refs[:-2], refs[-2:]
    shard = lax.axis_index("seq")
    delta = (total_ref[...] + head_sum(LAST, weight_ref, blocks)) * gate_ref[:, :1]
    for i in range(NSEQ):
        delta_ref[i] = delta[BLOCK * i : BLOCK * (i + 1)]
    for s in range(NSEQ):
        first = table_ref[0, s]
        counter = lax.rem(shard + NSEQ * NSEQ - first, NSEQ)
        for half in range(2):
            place = jnp.minimum((first + counter) // NSEQ + half, NSEQ - 1)
            out_ref[s, half] = delta_ref[place].astype(BF16)


def blend_kernel(table_ref, hot_ref, rows_ref, back_ref, out_hbm, update_ref, out_ref, sems):
    first = table_ref[0, lax.axis_index("seq")]
    for j in range(0, SLOTS // BLOCK, 2):
        pair = [
            back_ref[lax.rem(first + k, NSEQ), k // NSEQ].astype(F32) for k in (j, j + 1)
        ]
        update_ref[BLOCK * j : BLOCK * (j + 2)] = jnp.concatenate(pair, axis=0).astype(BF16)
    parts = out_ref.shape[0]
    wide = SRC // parts
    copies = []
    for p in range(parts):
        here = slice(wide * p, wide * (p + 1))
        added = jnp.dot(hot_ref[here], update_ref[...], preferred_element_type=F32)
        out_ref[p] = (rows_ref[here].astype(F32) + added).astype(BF16)
        copies.append(pltpu.make_async_copy(out_ref.at[p], out_hbm.at[pl.ds(wide * p, wide), :], sems.at[p]))
        copies[p].start()
    for copy in copies:
        copy.wait()


def z_step(array, steps):
    pairs = [(z * 2 + c, (z + steps) % 4 * 2 + c) for z in range(4) for c in range(2)]
    return lax.ppermute(array, "mp", pairs)


def other_core(array):
    return lax.ppermute(array, "mp", [(m, m ^ 1) for m in range(NMP)])


def hand_on_kernel(in_ref, token_ref, out_ref):
    out_ref[...] = in_ref[...]


def hand_on(array, token):
    return pl.pallas_call(
        hand_on_kernel,
        out_shape=pltpu.VMEM(array.shape, array.dtype),
        in_specs=[VMEM, ANY],
        out_specs=VMEM,
        compiler_params=params(4),
        name="hand_on",
    )(array, token)


def z_blocks(array):
    return {0: array, 2: z_step(array, 1), 6: z_step(array, 3), 4: z_step(array, 2)}


def add_cores(blocks, token):
    for k in (6, 2, 4):
        blocks[k + 1] = other_core(hand_on(blocks[k], token) if k == 6 else blocks[k])


def shape(dims, dtype=BF16):
    return jax.ShapeDtypeStruct(dims, dtype)


def on_device(
    residual_activations,
    prelayer_gain_vector,
    gating_projection,
    asker_projection,
    lookup_projection,
    content_projection,
    final_projection,
    logit_sharpness,
    selection_table,
    dispatched_tally_table,
):
    outgoing, table, sharpness = pl.pallas_call(
        pick_kernel,
        out_shape=(
            pltpu.VMEM((NSEQ, 2, BLOCK, FEAT), BF16),
            pltpu.SMEM((3, NSEQ), jnp.int32),
            pltpu.SMEM((GROUP,), F32),
        ),
        in_specs=[HBM] * 4,
        out_specs=(VMEM, SMEM, SMEM),
        scratch_shapes=[
            pltpu.VMEM((3, NSEQ), jnp.int32),
            pltpu.VMEM((NSEQ, NSEQ), jnp.int32),
            pltpu.VMEM((1, SLOTS), jnp.int32),
            pltpu.VMEM((4, SRC // 4, FEAT), BF16),
            pltpu.SemaphoreType.DMA((8,)),
        ],
        compiler_params=params(16),
        name="pick",
    )(
        in_hbm(dispatched_tally_table),
        in_hbm(selection_table),
        in_hbm(residual_activations),
        in_hbm(logit_sharpness),
    )
    incoming = lax.all_to_all(outgoing, "seq", split_axis=0, concat_axis=0, tiled=True)
    tokens = pl.pallas_call(
        compact_kernel,
        out_shape=shape((OWNED, FEAT)),
        in_specs=[SMEM, VMEM],
        out_specs=VMEM,
        compiler_params=params(4),
        name="compact",
    )(table, incoming)
    lookup, content, asker, loaded = pl.pallas_call(
        load_in_kernel,
        out_shape=(
            pltpu.VMEM((WIDTH, HEAD), BF16),
            pltpu.VMEM((WIDTH, HEAD), BF16),
            pltpu.VMEM((WIDTH, GROUP * HEAD), BF16),
            pltpu.VMEM((8, 128), F32),
        ),
        in_specs=[HBM] * 3 + [ANY],
        out_specs=[VMEM] * 4,
        scratch_shapes=[pltpu.SemaphoreType.DMA((12,))],
        compiler_params=params(8),
        name="load_in",
    )(in_hbm(lookup_projection), in_hbm(content_projection), in_hbm(asker_projection), tokens)
    blocks = z_blocks(tokens)
    blocks[1] = other_core(tokens)
    add_cores(blocks, loaded)
    blocks = [blocks[k] for k in range(NMP)]
    squares, gain = pl.pallas_call(
        square_kernel,
        out_shape=(pltpu.VMEM((OWNED, 128), F32), pltpu.VMEM((NMP, FEAT // 128, 128), F32)),
        in_specs=[VMEM] * 5,
        out_specs=(VMEM, VMEM),
        compiler_params=params(4),
        name="square",
    )(prelayer_gain_vector.reshape(WIDTH // 128, 128), *(blocks[k] for k in (0, 2, 4, 6)))
    query, pair = pl.pallas_call(
        project_in_kernel,
        out_shape=(
            pltpu.VMEM((OWNED, GROUP * HEAD), BF16),
            pltpu.VMEM((NSEQ, OWNED, 2 * HEAD), BF16),
        ),
        in_specs=[VMEM] * (5 + NMP),
        out_specs=[VMEM] * 2,
        compiler_params=params(16),
        cost_estimate=cost(2 * OWNED * WIDTH * 10 * HEAD, 4 * MIB),
        name="project_in",
    )(
        squares,
        gain,
        asker,
        lookup,
        content,
        *blocks,
    )
    pairs = lax.all_to_all(pair, "seq", split_axis=0, concat_axis=0, tiled=True)

    attended = pl.pallas_call(
        attention_kernel,
        out_shape=shape((OWNED, GROUP * HEAD)),
        in_specs=[SMEM, VMEM, VMEM],
        out_specs=VMEM,
        compiler_params=params(24),
        name="attend",
    )(sharpness, query, pairs)
    final, total, gate, hot = pl.pallas_call(
        load_out_kernel,
        out_shape=(
            pltpu.VMEM((NMP * GROUP * HEAD, FEAT), BF16),
            pltpu.VMEM((OWNED, FEAT), F32),
            pltpu.VMEM((OWNED, 128), F32),
            pltpu.VMEM((SRC, SLOTS), BF16),
        ),
        in_specs=[HBM] + [VMEM] * (4 + NMP),
        out_specs=[VMEM] * 4,
        scratch_shapes=[pltpu.VMEM((NMP, FEAT // 128, 128), F32), pltpu.SemaphoreType.DMA((8,))],
        compiler_params=params(8),
        name="load_out",
    )(
        in_hbm(final_projection),
        dispatched_tally_table,
        selection_table,
        gating_projection.reshape(WIDTH // 128, 128),
        attended,
        *blocks,
    )
    heads = z_blocks(attended)
    heads[1] = other_core(attended)
    add_cores(heads, total)
    total = pl.pallas_call(
        project_middle_kernel,
        out_shape=pltpu.VMEM((OWNED, FEAT), F32),
        in_specs=[VMEM] * (2 + len(MIDDLE)),
        out_specs=VMEM,
        compiler_params=params(16),
        name="project_middle",
    )(total, final, *(heads[k] for k in MIDDLE))
    outgoing_back = pl.pallas_call(
        project_last_kernel,
        out_shape=pltpu.VMEM((NSEQ, 2, BLOCK, FEAT), BF16),
        in_specs=[SMEM] + [VMEM] * (3 + len(LAST)),
        out_specs=VMEM,
        scratch_shapes=[pltpu.VMEM((NSEQ, BLOCK, FEAT), F32)],
        compiler_params=params(16),
        name="project_last",
    )(table, gate, total, final, *(heads[k] for k in LAST))
    back = lax.all_to_all(outgoing_back, "seq", split_axis=0, concat_axis=0, tiled=True)
    return pl.pallas_call(
        blend_kernel,
        out_shape=shape((SRC, FEAT)),
        in_specs=[SMEM] + [VMEM] * 3,
        out_specs=HBM,
        scratch_shapes=[
            pltpu.VMEM((SLOTS, FEAT), BF16),
            pltpu.VMEM((4, SRC // 4, FEAT), BF16),
            pltpu.SemaphoreType.DMA((4,)),
        ],
        compiler_params=params(16),
        name="blend",
    )(table, hot, residual_activations, back)


def solution(mesh):
    placed = (
        P("seq", "mp"),
        P(),
        P(),
        P(None, "mp"),
        P(None, "mp"),
        P(None, "mp"),
        P(None, "mp"),
        P("mp"),
        P("seq", None),
        P(),
    )
    return jax.shard_map(
        on_device, mesh=mesh, in_specs=placed, out_specs=P("seq", "mp"), check_vma=False
    )
```
